512 devices in a mesh: pre: 32 (over y, z_lo, core), rep: 16 (over z_hi, x).
Axes of the slice: x: 4, y: 8, z: 8 (z_hi: 4, z_lo: 2; z = z_hi * 2 + z_lo), core: 2. Of those that a mesh axis runs over, the one named last changes fastest.
Arguments:
- grads: bfloat16 [32, 32, 512, 512], P('rep', 'pre')
- owner: int32 [32], replicated, may hold values from 0 to 31, as said below
- state: float32 [32, 2, 512, 512], P('pre', None, 'rep'), as said below
Outputs:
- new_state: float32 [32, 2, 512, 512], P('pre', None, 'rep')
- update: bfloat16 [32, 512, 512], P('pre', 'rep')
The draws below stay inside these ranges and needn't reach their ends.
Inputs may be any that keep to these rules, and one draw needn't show every extreme that they name: Each owner index is named by at most 2 blocks, and some owner by exactly 2. `state`: each matrix is symmetric.
All inputs are finite; a program needn't handle non-finite values.
Results may differ from the reference program's by a relative error of at most 0.006.
Values sent between devices are 32-bit elements; how exact they have to be, the bound alone decides.
No kernel may reach another device: no remote copies, remote signals or barrier semaphores. Data moves between devices by JAX's collectives and lax.ppermute only.
A program may use at most 64 MiB of HBM per device.

```python
import math
import jax
import jax.numpy as jnp
from jax import lax

K = 512
CAP = 2
ITERS = 4
NB = 32
SHARDS = 32
N_PRE = 32


def draw_grads(key, part):
    key = jax.random.fold_in(key, 11)
    keys = jax.random.split(key, 3)
    row_scale = jnp.exp(jax.random.uniform(keys[0], (1, NB, K, 1)) * math.log(10.0))
    shard_scale = 3.0 ** (jnp.arange(SHARDS, dtype=jnp.float32) / (SHARDS - 1))
    common = jax.random.normal(keys[1], (1, NB, K, K))
    noise = jax.random.normal(keys[2], (SHARDS, NB, K, K))
    values = 3.0 * row_scale * (common + shard_scale[:, None, None, None] * noise)
    return values.astype(jnp.bfloat16)


def draw_owner(key, part):
    key = jax.random.fold_in(key, 17)
    keys = jax.random.split(key, 2)
    first = jax.random.randint(keys[0], (), 0, N_PRE).astype(jnp.int32)
    shared = (first + N_PRE - 1) % N_PRE
    second = (first + 1) % N_PRE
    others = (shared + 1 + jnp.arange(N_PRE - 1, dtype=jnp.int32)) % N_PRE
    others = others[jax.random.permutation(keys[1], N_PRE - 1)]
    rest = (first + 2 + jnp.arange(N_PRE - 2, dtype=jnp.int32)) % N_PRE
    result = jnp.zeros((NB,), jnp.int32)
    result = result.at[rest].set(others[:N_PRE - 2])
    result = result.at[first].set(shared)
    result = result.at[second].set(shared)
    return result


def draw_state(key, part):
    key = jax.random.fold_in(key, 23)
    keys = jax.random.split(key, 3)
    spread = jax.random.uniform(keys[0], (N_PRE, CAP, K))
    base = 10.0 * K * SHARDS
    position = jnp.arange(K, dtype=jnp.float32) / (K - 1)
    diagonal = base * jnp.exp(spread * math.log(100.0)) * 3.0 ** position
    places = jax.random.uniform(keys[1], (N_PRE, CAP, K)) * K
    signs = (2 * jax.random.randint(keys[2], (N_PRE, CAP, K), 0, 2) - 1).astype(jnp.float32)
    kernel = jnp.exp(-jnp.abs(places[..., :, None] - places[..., None, :]) / 8.0)
    coupling = signs[..., :, None] * signs[..., None, :] * kernel
    rooted = jnp.sqrt(diagonal)
    identity = jnp.eye(K, dtype=jnp.float32)
    return rooted[..., :, None] * rooted[..., None, :] * (identity + 0.8 * coupling)


def setup_inputs(seed: int = 0) -> dict:
    arg_keys = jax.random.split(jax.random.key(seed), 4)
    return {
        "grads": draw_grads(jax.random.fold_in(arg_keys[3], 71), 0),
        "owner": draw_owner(jax.random.fold_in(arg_keys[3], 71), 0),
        "state": draw_state(jax.random.fold_in(arg_keys[3], 71), 0),
    }


DAMP = 0.05

def root_iterate(stat):
    order_size = stat.shape[0]
    identity = jnp.eye(order_size, dtype=jnp.float32)
    norm_stat = jnp.sqrt(jnp.sum(stat * stat))
    damped = stat + DAMP * norm_stat * identity
    scale_norm = jnp.sqrt(jnp.sum(damped * damped))
    iterate = damped / scale_norm
    root_block = scale_norm ** (-0.25) * identity
    for rounds in range(ITERS):
        factor = (5.0 * identity - iterate) * 0.25
        root_block = jnp.dot(root_block, factor, precision=lax.Precision.HIGHEST)
        if rounds + 1 < ITERS:
            for repeat in range(4):
                iterate = jnp.dot(iterate, factor, precision=lax.Precision.HIGHEST)
    return root_block

def reference(grads, owner, state):
    block_ids = jnp.arange(NB, dtype=jnp.int32)
    earlier = (owner[None, :] == owner[:, None]) & (block_ids[None, :] < block_ids[:, None])
    slot_of = lax.optimization_barrier(jnp.sum(earlier.astype(jnp.int32), axis=1))

    def gram_of(block_id):
        shards = lax.dynamic_index_in_dim(grads, block_id, 1, keepdims=False)
        return lax.dot_general(shards, shards, (((0, 2), (0, 2)), ((), ())), preferred_element_type=jnp.float32)
    gram_all = lax.map(gram_of, block_ids)
    owner_ids = jnp.arange(N_PRE, dtype=jnp.int32)
    slot_ids = jnp.arange(CAP, dtype=jnp.int32)
    select = ((owner[None, None, :] == owner_ids[:, None, None]) & (slot_of[None, None, :] == slot_ids[None, :, None])).astype(jnp.float32)
    new_state = state + jnp.einsum('osb,bij->osij', select, gram_all, precision=lax.Precision.HIGHEST)
    stat_all = new_state[owner, slot_of]
    root_all = lax.map(root_iterate, stat_all)

    def apply_block(block_id):
        shards = lax.dynamic_index_in_dim(grads, block_id, 1, keepdims=False)
        mean_grad = (lax.optimization_barrier(jnp.sum(shards.astype(jnp.float32), axis=0)) / SHARDS).astype(jnp.bfloat16)
        precond = lax.dynamic_index_in_dim(root_all, block_id, 0, keepdims=False).astype(jnp.bfloat16)
        return jnp.dot(precond, mean_grad, preferred_element_type=jnp.float32).astype(jnp.bfloat16)
    update = lax.map(apply_block, block_ids)
    return (new_state, update)
```

```python
import jax
import jax.numpy as jnp
from jax import lax
from jax.experimental import pallas as pl
from jax.experimental.pallas import tpu as pltpu
from jax.sharding import PartitionSpec as P

ITERS = 4
DAMP = 0.05
GROUP = 4
f32 = jnp.float32
bf16 = jnp.bfloat16

VMEM = pl.BlockSpec(memory_space=pltpu.VMEM)
SMEM = pl.BlockSpec(memory_space=pltpu.SMEM)
PARAMS = pltpu.CompilerParams(vmem_limit_bytes=40 * 2**20)


def call(kernel, out_shape, in_specs, cost, *args):
    multiple = isinstance(out_shape, (list, tuple))
    return pl.pallas_call(
        kernel,
        out_shape=out_shape,
        in_specs=in_specs,
        out_specs=[VMEM] * len(out_shape) if multiple else VMEM,
        compiler_params=PARAMS,
        cost_estimate=pl.CostEstimate(flops=cost[0], bytes_accessed=cost[1], transcendentals=0),
    )(*args)


def gram_kernel(grads_ref, gram_ref, total_ref):
    shards, size, _ = grads_ref.shape
    parts = gram_ref.shape[0]
    rows = size // parts
    gram = None
    total = None
    for s in range(shards):
        g = grads_ref[s]
        term = lax.dot_general(g, g, (((1,), (1,)), ((), ())), preferred_element_type=f32)
        gram = term if gram is None else gram + term
        wide = g.astype(f32)
        total = wide if total is None else total + wide
    gram_ref[...] = gram.reshape(parts, rows, size)
    total_ref[...] = total.reshape(parts, rows, size)


def choose(k, options):
    value = options[0]
    for i in range(1, len(options)):
        value = jnp.where(k == i, options[i], value)
    return value


def spread_kernel(where_ref, held0, held1, held2, held3, out_ref):
    held = (held0, held1, held2, held3)
    for y in range(out_ref.shape[0]):
        k = where_ref[0, y]
        j = where_ref[1, y]
        out_ref[y] = choose(k, [h[pl.ds(j, 1)][0] for h in held])


def stat_kernel(source_ref, gram_ref, state_ref, wide_ref, owner_ref):
    stat = jnp.sum(gram_ref[...], axis=0) + state_ref[pl.ds(source_ref[0], 1)][0]
    wide_ref[...] = jnp.broadcast_to(stat[None], wide_ref.shape)
    owner_ref[...] = jnp.broadcast_to(stat[None], owner_ref.shape)


def total_kernel(total_ref, wide_ref):
    wide_ref[...] = jnp.broadcast_to(jnp.sum(total_ref[...], axis=0)[None], wide_ref.shape)


def return_kernel(source_ref, rows_ref, out0, out1, out2, out3):
    for k, out in enumerate((out0, out1, out2, out3)):
        for j in range(out.shape[0]):
            out[j] = rows_ref[pl.ds(source_ref[k, j], 1)][0]


def state_kernel(sender_ref, state_ref, got0, got1, got2, got3, out_ref):
    for j in range(out_ref.shape[0]):
        out_ref[j] = choose(
            sender_ref[j], [got0[j], got1[j], got2[j], got3[j], state_ref[j]]
        )


def product(a, b):
    a_high = a.astype(bf16)
    a_low = (a - a_high.astype(f32)).astype(bf16)
    b_high = b.astype(bf16)
    b_low = (b - b_high.astype(f32)).astype(bf16)
    return jnp.dot(
        jnp.concatenate([a_high, a_high, a_low], axis=1),
        jnp.concatenate([b_high, b_low, b_high], axis=0),
        preferred_element_type=f32,
    )


def newton_kernel(place_ref, stat_ref, root_ref):
    parts, rows, size = stat_ref.shape
    stat = stat_ref[...].reshape(size, size)
    row_ids = lax.broadcasted_iota(jnp.int32, (size, size), 0)
    col_ids = lax.broadcasted_iota(jnp.int32, (size, size), 1)
    eye = (row_ids == col_ids).astype(f32)
    norm = jnp.sqrt(jnp.sum(stat * stat))
    damped = stat + (DAMP * norm) * eye
    scale = jnp.sqrt(jnp.sum(damped * damped))
    iterate = damped / scale
    root = 1.25 * eye - 0.25 * iterate
    for _ in range(1, ITERS):
        square = product(iterate, iterate)
        factor2 = 1.5625 * eye - 0.625 * iterate + 0.0625 * square
        iterate = product(iterate, product(factor2, factor2))
        root = 1.25 * root - 0.25 * product(root, iterate)
    root = (root * jnp.exp(-0.25 * jnp.log(scale))).astype(bf16)
    root_ref[...] = root.reshape(parts, rows, size)


def update_kernel(count, place_ref, root_ref, total_ref, out_ref):
    parts, rows, size = total_ref.shape
    mean = (total_ref[...].reshape(size, size) / count).astype(bf16)
    mine = root_ref[pl.ds(place_ref[0], 1)][0]
    out_ref[0] = jnp.dot(mine, mean, preferred_element_type=f32).astype(bf16)


def body(grads, owner, state):
    local = grads[:, 0]
    shards, size, _ = local.shape
    held = state[0]
    capacity, rows, _ = held.shape
    reps = lax.axis_size("rep")
    blocks = owner.shape[0]
    groups = blocks // GROUP
    shape = lambda *s: jax.ShapeDtypeStruct(s, f32)

    me = lax.axis_index("pre")
    my_y, my_q = me // GROUP, me % GROUP
    place = lax.axis_index("rep").reshape(1).astype(jnp.int32)
    ids = jnp.arange(blocks, dtype=jnp.int32)
    slot = jnp.sum(
        ((owner[None, :] == owner[:, None]) & (ids[None, :] < ids[:, None])).astype(jnp.int32), axis=1
    )
    mine = ids % GROUP == my_q
    by_y = lambda v: jnp.sum(
        jnp.where(mine[None, :] & (ids[None, :] // GROUP == jnp.arange(groups)[:, None]), v[None, :], 0), axis=1
    )
    wanted, wanted_slot = by_y(owner), by_y(slot)
    where = jnp.stack([(wanted % GROUP) ^ my_q, wanted_slot]).astype(jnp.int32)
    my_owner = jnp.sum(jnp.where(ids == me, owner, 0))
    source = (my_owner // GROUP).reshape(1).astype(jnp.int32)
    q_ids = jnp.arange(GROUP, dtype=jnp.int32)
    targets = my_y * GROUP + (q_ids ^ my_q)
    slots = jnp.arange(capacity, dtype=jnp.int32)
    block_of = jnp.max(
        jnp.where(
            (owner[None, None, :] == targets[:, None, None]) & (slot[None, None, :] == slots[None, :, None]),
            ids[None, None, :],
            -1,
        ),
        axis=2,
    )
    return_source = jnp.maximum(block_of, 0) // GROUP
    sender = jnp.where(block_of[0] >= 0, (block_of[0] % GROUP) ^ my_q, GROUP).astype(jnp.int32)

    def across(x, k):
        return lax.ppermute(x, "pre", [(i, i ^ k) for i in range(blocks)])

    y_groups = [[y * GROUP + q for y in range(groups)] for q in range(GROUP)]

    gram, total = call(
        gram_kernel,
        [shape(reps, rows, size), shape(reps, rows, size)],
        [VMEM],
        (2 * shards * size**3, 4 * size * size * (shards + 2)),
        local,
    )
    gram = lax.all_to_all(gram, "rep", 0, 0, tiled=True)
    shared = [held] + [across(held, k) for k in range(1, GROUP)]
    chosen = call(
        spread_kernel,
        shape(groups, rows, size),
        [SMEM] + [VMEM] * GROUP,
        (0, 4 * size * rows * 16),
        where,
        *shared,
    )
    chosen = lax.all_to_all(chosen, "pre", 0, 0, tiled=True, axis_index_groups=y_groups)
    stat, outgoing = call(
        stat_kernel,
        [shape(reps, rows, size), shape(groups, rows, size)],
        [SMEM, VMEM, VMEM],
        (0, 4 * size * rows * 48),
        source,
        gram,
        chosen,
    )
    stat = lax.all_to_all(stat, "rep", 0, 0, tiled=True)
    total = lax.all_to_all(total, "rep", 0, 0, tiled=True)
    total = call(
        total_kernel, shape(reps, rows, size), [VMEM], (0, 4 * size * rows * 32), total
    )
    total = lax.all_to_all(total, "rep", 0, 0, tiled=True)
    outgoing = lax.all_to_all(outgoing, "pre", 0, 0, tiled=True, axis_index_groups=y_groups)
    returned = call(
        return_kernel,
        [shape(capacity, rows, size)] * GROUP,
        [SMEM, VMEM],
        (0, 4 * size * rows * 16),
        return_source.astype(jnp.int32),
        outgoing,
    )
    returned = [returned[0]] + [across(returned[k], k) for k in range(1, GROUP)]
    new_state = call(
        state_kernel,
        shape(capacity, rows, size),
        [SMEM] + [VMEM] * (GROUP + 1),
        (0, 4 * size * rows * 12),
        sender,
        held,
        *returned,
    )
    root = call(
        newton_kernel,
        jax.ShapeDtypeStruct((reps, rows, size), bf16),
        [SMEM, VMEM],
        (2 * 36 * size**3, 6 * size * size),
        place,
        stat,
    )
    count = shards * reps
    update = call(
        lambda *refs: update_kernel(count, *refs),
        jax.ShapeDtypeStruct((1, rows, size), bf16),
        [SMEM, VMEM, VMEM],
        (2 * rows * size * size, 6 * size * size),
        place,
        root,
        total,
    )
    return (new_state[None], update)


def solution(mesh):
    placed = (P("rep", "pre", None, None), P(), P("pre", None, "rep", None))
    return jax.shard_map(
        body,
        mesh=mesh,
        in_specs=placed,
        out_specs=(P("pre", None, "rep", None), P("pre", "rep", None)),
        check_vma=False,
    )
```

```python
import jax
import jax.numpy as jnp
from jax import lax
from jax.experimental import pallas as pl
from jax.experimental.pallas import tpu as pltpu
from jax.sharding import PartitionSpec as P

ITERS = 4
DAMP = 0.05
GROUP = 4
f32 = jnp.float32
bf16 = jnp.bfloat16

VMEM = pl.BlockSpec(memory_space=pltpu.VMEM)
SMEM = pl.BlockSpec(memory_space=pltpu.SMEM)
PARAMS = pltpu.CompilerParams(vmem_limit_bytes=40 * 2**20)


def call(kernel, out_shape, in_specs, cost, *args):
    multiple = isinstance(out_shape, (list, tuple))
    return pl.pallas_call(
        kernel,
        out_shape=out_shape,
        in_specs=in_specs,
        out_specs=[VMEM] * len(out_shape) if multiple else VMEM,
        compiler_params=PARAMS,
        cost_estimate=pl.CostEstimate(flops=cost[0], bytes_accessed=cost[1], transcendentals=0),
    )(*args)


def gram_kernel(grads_ref, out_ref):
    shards, size, _ = grads_ref.shape
    parts = out_ref.shape[0]
    rows = size // parts
    gram = None
    total = None
    for s in range(shards):
        g = grads_ref[s]
        term = lax.dot_general(g, g, (((1,), (1,)), ((), ())), preferred_element_type=f32)
        gram = term if gram is None else gram + term
        wide = g.astype(f32)
        total = wide if total is None else total + wide
    out_ref[:, :rows, :] = gram.reshape(parts, rows, size)
    out_ref[:, rows:, :] = total.T.reshape(parts, rows, size)


def choose(k, options):
    value = options[0]
    for i in range(1, len(options)):
        value = jnp.where(k == i, options[i], value)
    return value


def spread_kernel(where_ref, held_ref, out0, out1, out2, out3):
    for k, out in enumerate((out0, out1, out2, out3)):
        out[...] = held_ref[where_ref[0, k], where_ref[1, k]]


def stat_kernel(sender_ref, sums_ref, state0, state1, state2, state3, wide_ref, owner_ref, total_ref):
    rows = state0.shape[0]
    sums = jnp.sum(sums_ref[...], axis=0)
    state = choose(sender_ref[0], [s[...] for s in (state0, state1, state2, state3)])
    stat = sums[:rows] + state
    wide_ref[...] = jnp.broadcast_to(stat[None], wide_ref.shape)
    owner_ref[0] = stat
    owner_ref[1] = stat
    total_ref[...] = sums[rows:]


def return_kernel(source_ref, rows_ref, out0, out1, out2, out3):
    for k, out in enumerate((out0, out1, out2, out3)):
        for j in range(out.shape[0]):
            out[j] = rows_ref[source_ref[k, j], 0]


def state_kernel(sender_ref, state_ref, got0, got1, got2, got3, out_ref):
    for j in range(out_ref.shape[0]):
        out_ref[j] = choose(
            sender_ref[j], [got0[j], got1[j], got2[j], got3[j], state_ref[j]]
        )


def split(a):
    high = a.astype(bf16)
    return high, (a - high.astype(f32)).astype(bf16)


def product(a, b):
    (a_high, a_low), (b_high, b_low) = a, b
    dot = lambda x, y: jnp.dot(x, y, preferred_element_type=f32)
    return dot(a_high, b_high) + (dot(a_high, b_low) + dot(a_low, b_high))


def newton_kernel(count, stat_ref, total_ref, out_ref):
    parts, rows, size = stat_ref.shape
    stat = stat_ref[...].reshape(size, size)
    row_ids = lax.broadcasted_iota(jnp.int32, (size, size), 0)
    col_ids = lax.broadcasted_iota(jnp.int32, (size, size), 1)
    eye = (row_ids == col_ids).astype(f32)
    norm = jnp.sqrt(jnp.sum(stat * stat))
    damped = stat + (DAMP * norm) * eye
    scale = jnp.sqrt(jnp.sum(damped * damped))
    iterate = damped / scale
    thin = (total_ref[...] / count).astype(bf16).astype(f32)
    for rounds in range(ITERS - 1):
        parts_of = split(iterate)
        thin = 1.25 * thin - 0.25 * product(split(thin), parts_of)
        if rounds + 2 < ITERS:
            square = product(parts_of, parts_of)
            factor2 = split(1.5625 * eye - 0.625 * iterate + 0.0625 * square)
            iterate = product(parts_of, split(product(factor2, factor2)))
    last = product(split(thin), parts_of)
    for _ in range(4):
        last = 1.25 * last - 0.25 * product(split(last), parts_of)
    thin = (1.25 * thin - 0.25 * last) * jnp.exp(-0.25 * jnp.log(scale))
    groups = out_ref.shape[2] // rows
    tall = thin.T.reshape(parts, groups, rows // groups, rows)
    out_ref[...] = jnp.concatenate([tall[:, i] for i in range(groups)], axis=2)


def update_kernel(got_ref, out_ref):
    _, rows, size = out_ref.shape
    parts, height, width = got_ref.shape
    groups = width // rows
    for i in range(groups):
        strip = jnp.concatenate([got_ref[r][:, i * rows : (i + 1) * rows] for r in range(parts)], axis=1)
        out_ref[0, i * height : (i + 1) * height, :] = strip.astype(bf16)


def body(grads, owner, state):
    local = grads[:, 0]
    shards, size, _ = local.shape
    held = state[0]
    capacity, rows, _ = held.shape
    reps = lax.axis_size("rep")
    blocks = owner.shape[0]
    groups = blocks // GROUP
    shape = lambda *s: jax.ShapeDtypeStruct(s, f32)
    y_groups = [[y * GROUP + q for y in range(groups)] for q in range(GROUP)]

    def across(x, k):
        return lax.ppermute(x, "pre", [(i, i ^ k) for i in range(blocks)])

    def over_y(x):
        return lax.all_gather(x, "pre", axis=0, axis_index_groups=y_groups)

    me = lax.axis_index("pre")
    my_y, my_q = me // GROUP, me % GROUP
    ids = jnp.arange(blocks, dtype=jnp.int32)
    slot = jnp.sum(
        ((owner[None, :] == owner[:, None]) & (ids[None, :] < ids[:, None])).astype(jnp.int32), axis=1
    )
    partners = my_y * GROUP + (jnp.arange(GROUP, dtype=jnp.int32) ^ my_q)
    at_partner = lambda v: jnp.sum(jnp.where(ids[None, :] == partners[:, None], v[None, :], 0), axis=1)
    wanted = at_partner(owner)
    where = jnp.stack([wanted // GROUP, at_partner(slot)]).astype(jnp.int32)
    state_sender = ((wanted[:1] % GROUP) ^ my_q).astype(jnp.int32)
    slots = jnp.arange(capacity, dtype=jnp.int32)
    block_of = jnp.max(
        jnp.where(
            (owner[None, None, :] == partners[:, None, None]) & (slot[None, None, :] == slots[None, :, None]),
            ids[None, None, :],
            -1,
        ),
        axis=2,
    )
    return_source = (jnp.maximum(block_of, 0) // GROUP).astype(jnp.int32)
    stat_sender = jnp.where(block_of[0] >= 0, (block_of[0] % GROUP) ^ my_q, GROUP).astype(jnp.int32)

    all_held = over_y(held)
    sums = call(
        gram_kernel,
        shape(reps, 2 * rows, size),
        [VMEM],
        (2 * shards * size**3, 4 * size * size * (shards + 2)),
        local,
    )
    sums = lax.all_to_all(sums, "rep", 0, 0, tiled=True)
    sent = call(
        spread_kernel,
        [shape(rows, size)] * GROUP,
        [SMEM, VMEM],
        (0, 4 * size * rows * 8),
        where,
        all_held,
    )
    got = [sent[0]] + [across(sent[k], k) for k in range(1, GROUP)]
    stat, outgoing, total = call(
        stat_kernel,
        [shape(reps, rows, size), shape(2, rows, size), shape(rows, size)],
        [SMEM] + [VMEM] * (GROUP + 1),
        (0, 4 * size * rows * 48),
        state_sender,
        sums,
        *got,
    )
    stat = lax.all_to_all(stat, "rep", 0, 0, tiled=True)
    outgoing = over_y(outgoing)
    count = shards * reps
    groups_of = 128 // rows
    columns = call(
        lambda *refs: newton_kernel(count, *refs),
        shape(reps, rows // groups_of, groups_of * rows),
        [VMEM, VMEM],
        (2 * 20 * size**3, 4 * size * size),
        stat,
        total,
    )
    columns = lax.all_to_all(columns, "rep", 0, 0, tiled=True)
    returned = call(
        return_kernel,
        [shape(capacity, rows, size)] * GROUP,
        [SMEM, VMEM],
        (0, 4 * size * rows * 16),
        return_source,
        outgoing,
    )
    returned = [returned[0]] + [across(returned[k], k) for k in range(1, GROUP)]
    new_state = call(
        state_kernel,
        shape(capacity, rows, size),
        [SMEM] + [VMEM] * (GROUP + 1),
        (0, 4 * size * rows * 12),
        stat_sender,
        held,
        *returned,
    )
    update = call(
        update_kernel,
        jax.ShapeDtypeStruct((1, rows, size), bf16),
        [VMEM],
        (0, 6 * rows * size),
        columns,
    )
    return (new_state[None], update)


def solution(mesh):
    placed = (P("rep", "pre", None, None), P(), P("pre", None, "rep", None))
    return jax.shard_map(
        body,
        mesh=mesh,
        in_specs=placed,
        out_specs=(P("pre", None, "rep", None), P("pre", "rep", None)),
        check_vma=False,
    )
```

```python
import jax
import jax.numpy as jnp
from jax import lax
from jax.experimental import pallas as pl
from jax.experimental.pallas import tpu as pltpu
from jax.sharding import PartitionSpec as P

ITERS = 4
DAMP = 0.05
GROUP = 4
ACROSS = 4
f32 = jnp.float32
bf16 = jnp.bfloat16

VMEM = pl.BlockSpec(memory_space=pltpu.VMEM)
ANY = pl.BlockSpec(memory_space=pl.ANY)
SMEM = pl.BlockSpec(memory_space=pltpu.SMEM)
PARAMS = pltpu.CompilerParams(vmem_limit_bytes=40 * 2**20)


def call(kernel, out_shape, in_specs, cost, *args, scratch=()):
    multiple = isinstance(out_shape, (list, tuple))
    return pl.pallas_call(
        kernel,
        out_shape=out_shape,
        in_specs=in_specs,
        out_specs=[VMEM] * len(out_shape) if multiple else VMEM,
        scratch_shapes=list(scratch),
        compiler_params=PARAMS,
        cost_estimate=pl.CostEstimate(flops=cost[0], bytes_accessed=cost[1], transcendentals=0),
    )(*args)


def gram_kernel(grads_ref, out_ref):
    shards, size, _ = grads_ref.shape
    xs, zs, double, _ = out_ref.shape
    rows = double // 2
    gram = None
    total = None
    for s in range(shards):
        g = grads_ref[s]
        term = lax.dot_general(g, g, (((1,), (1,)), ((), ())), preferred_element_type=f32)
        gram = term if gram is None else gram + term
        wide = g.astype(f32)
        total = wide if total is None else total + wide
    gram = gram.reshape(zs, xs, rows, size)
    total = total.reshape(zs, xs, rows, size)
    for x in range(xs):
        out_ref[x, :, :rows, :] = gram[:, x]
        out_ref[x, :, rows:, :] = total[:, x]


def sum_kernel(parts_ref, after_ref, out_ref):
    del after_ref
    out_ref[...] = jnp.sum(parts_ref[...], axis=0)


def choose(k, options):
    value = options[0]
    for i in range(1, len(options)):
        value = jnp.where(k == i, options[i], value)
    return value


def spread_kernel(where_ref, *refs):
    held, outs = refs[:GROUP], refs[GROUP:]
    for y, out in enumerate(outs):
        j = where_ref[1, y]
        out[...] = choose(where_ref[0, y], [h[j] for h in held])


def stat_kernel(sender_ref, sums_ref, *refs):
    states, (wide_ref, gram_ref) = refs[:-2], refs[-2:]
    parts, _, _ = wide_ref.shape
    rows = gram_ref.shape[0]
    sums = jnp.sum(sums_ref[...], axis=0)
    gram_ref[...] = sums[:rows]
    stat = sums[:rows] + choose(sender_ref[0], [s[...] for s in states])
    both = jnp.concatenate([stat, sums[rows:]], axis=0)
    wide_ref[...] = jnp.broadcast_to(both[None], wide_ref.shape)


def return_kernel(source_ref, gram0, gram1, gram2, gram3, after_ref, out_ref):
    del after_ref
    grams = (gram0, gram1, gram2, gram3)
    ys, capacity, _, _ = out_ref.shape
    for y in range(ys):
        for j in range(capacity):
            out_ref[y, j] = choose(source_ref[y * capacity + j], [g[...] for g in grams])


def state_kernel(source_ref, state_ref, got_ref, after_ref, out_ref):
    del after_ref
    for j in range(out_ref.shape[0]):
        y = source_ref[j]
        gram = got_ref[jnp.maximum(y, 0), j]
        out_ref[j] = state_ref[j] + jnp.where(y >= 0, gram, 0.0)


def split(a):
    high = a.astype(bf16)
    return high, (a - high.astype(f32)).astype(bf16)


def product(a, b):
    (a_high, a_low), (b_high, b_low) = a, b
    dot = lambda x, y: jnp.dot(x, y, preferred_element_type=f32)
    return dot(a_high, b_high) + (dot(a_high, b_low) + dot(a_low, b_high))


def assemble(place, refs, whole_ref):
    for k, ref in enumerate(refs):
        x = (place + ACROSS - k) % ACROSS
        for z in range(ref.shape[0]):
            whole_ref[z * ACROSS + x] = ref[z]


def newton_kernel(place_ref, *refs):
    stat_refs, (out_ref, stat_ref) = refs[:ACROSS], refs[ACROSS:]
    parts, rows, size = stat_ref.shape
    place = place_ref[0]
    assemble(place, stat_refs, stat_ref)
    stat = stat_ref[...].reshape(size, size)
    row_ids = lax.broadcasted_iota(jnp.int32, (size, size), 0)
    col_ids = lax.broadcasted_iota(jnp.int32, (size, size), 1)
    eye = (row_ids == col_ids).astype(f32)
    thin_rows = lax.broadcasted_iota(jnp.int32, (rows, size), 0) + place * rows
    thin_cols = lax.broadcasted_iota(jnp.int32, (rows, size), 1)
    thin_eye = (thin_rows == thin_cols).astype(f32)
    norm = jnp.sqrt(jnp.sum(stat * stat))
    damped = stat + (DAMP * norm) * eye
    scale = jnp.sqrt(jnp.sum(damped * damped))
    iterate = damped / scale
    mine = (stat_ref[place] + (DAMP * norm) * thin_eye) / scale
    thin = 1.25 * thin_eye - 0.25 * mine
    parts_of = split(iterate)
    for _ in range(ITERS - 2):
        square = product(parts_of, parts_of)
        factor2 = split(1.5625 * eye - 0.625 * iterate + 0.0625 * square)
        iterate = product(parts_of, split(product(factor2, factor2)))
        parts_of = split(iterate)
        thin = 1.25 * thin - 0.25 * product(split(thin), parts_of)
    last = product(split(thin), parts_of)
    for _ in range(4):
        last = 1.25 * last - 0.25 * product(split(last), parts_of)
    thin = (1.25 * thin - 0.25 * last) * jnp.exp(-0.25 * jnp.log(scale))
    out_ref[...] = thin.astype(bf16)


def update_kernel(count, place_ref, root_ref, *refs):
    total_refs, (out_ref, total_ref) = refs[:ACROSS], refs[ACROSS:]
    _, _, size = total_ref.shape
    assemble(place_ref[0], total_refs, total_ref)
    mean = (total_ref[...].reshape(size, size) / count).astype(bf16)
    out_ref[0] = jnp.dot(root_ref[...], mean, preferred_element_type=f32).astype(bf16)


def body(grads, owner, state):
    local = grads[:, 0]
    shards, size, _ = local.shape
    held = state[0]
    capacity, rows, _ = held.shape
    reps = lax.axis_size("rep")
    blocks = owner.shape[0]
    groups = blocks // GROUP
    shape = lambda *s: jax.ShapeDtypeStruct(s, f32)

    def across(x, k):
        return lax.ppermute(x, "pre", [(i, i ^ k) for i in range(blocks)])

    def along_y(x, k):
        return lax.ppermute(x, "pre", [(i, (i + k * GROUP) % blocks) for i in range(blocks)])

    def along_x(x, k):
        return lax.ppermute(
            x, "rep", [(i, i // ACROSS * ACROSS + (i + k) % ACROSS) for i in range(reps)]
        )

    zs = reps // ACROSS
    y_groups = [[y * GROUP + q for y in range(groups)] for q in range(GROUP)]
    x_groups = [[z * ACROSS + x for x in range(ACROSS)] for z in range(zs)]
    z_groups = [[z * ACROSS + x for z in range(zs)] for x in range(ACROSS)]

    def exchange(x, which):
        return lax.all_to_all(x, "rep", 0, 0, tiled=True, axis_index_groups=which)

    me = lax.axis_index("pre")
    my_y, my_q = me // GROUP, me % GROUP
    place = lax.axis_index("rep").reshape(1).astype(jnp.int32)
    ids = jnp.arange(blocks, dtype=jnp.int32)
    slot = jnp.sum(
        ((owner[None, :] == owner[:, None]) & (ids[None, :] < ids[:, None])).astype(jnp.int32), axis=1
    )
    ahead = (me + GROUP * jnp.arange(groups, dtype=jnp.int32)) % blocks
    at_ahead = lambda v: jnp.sum(jnp.where(ids[None, :] == ahead[:, None], v[None, :], 0), axis=1)
    wanted = at_ahead(owner)
    where = jnp.stack([(wanted % GROUP) ^ my_q, at_ahead(slot)]).astype(jnp.int32)
    state_sender = ((my_y - wanted[:1] // GROUP) % groups).astype(jnp.int32)
    slots = jnp.arange(capacity, dtype=jnp.int32)
    plane = jnp.arange(groups, dtype=jnp.int32) * GROUP + my_q
    block_of = jnp.max(
        jnp.where(
            (owner[None, None, :] == plane[:, None, None]) & (slot[None, None, :] == slots[None, :, None]),
            ids[None, None, :],
            -1,
        ),
        axis=2,
    )
    return_source = ((block_of % GROUP) ^ my_q).reshape(-1).astype(jnp.int32)
    mine = jnp.max(jnp.where(plane[:, None] == me, block_of, -1), axis=0)
    stat_source = jnp.where(mine >= 0, mine // GROUP, -1).astype(jnp.int32)

    held_z = across(held, 2)
    sums = call(
        gram_kernel,
        shape(ACROSS, zs, 2 * rows, size),
        [VMEM],
        (2 * shards * size**3, 4 * size * size * (shards + 2)),
        local,
    )
    sums = exchange(sums, x_groups)
    sent = call(
        spread_kernel,
        [shape(rows, size)] * groups,
        [SMEM] + [VMEM] * GROUP,
        (0, 4 * size * rows * 16),
        where,
        held,
        across(held, 1),
        held_z,
        across(held_z, 1),
    )
    sums = call(
        sum_kernel,
        shape(zs, 2 * rows, size),
        [VMEM, ANY],
        (0, 4 * size * rows * 40),
        sums,
        sent[0],
    )
    sums = exchange(sums, z_groups)
    got = [sent[0]] + [along_y(sent[k], k) for k in range(1, groups)]
    both, gram = call(
        stat_kernel,
        [shape(zs, 2 * rows, size), shape(rows, size)],
        [SMEM] + [VMEM] * (groups + 1),
        (0, 4 * size * rows * 25),
        state_sender,
        sums,
        *got,
    )
    both = exchange(both, z_groups)
    stat, total = both[:, :rows], both[:, rows:]
    stats = [stat] + [along_x(stat, k) for k in range(1, ACROSS)]
    totals = [total] + [along_x(total, k) for k in range(1, ACROSS)]
    returned = call(
        return_kernel,
        shape(groups, capacity, rows, size),
        [SMEM] + [VMEM] * GROUP + [ANY],
        (0, 4 * size * rows * 20),
        return_source,
        gram,
        *[across(gram, k) for k in range(1, GROUP)],
        both,
    )
    returned = lax.all_to_all(returned, "pre", 0, 0, tiled=True, axis_index_groups=y_groups)
    count = shards * reps
    root = call(
        newton_kernel,
        jax.ShapeDtypeStruct((rows, size), bf16),
        [SMEM] + [VMEM] * ACROSS,
        (2 * 20 * size**3, 4 * size * size),
        place,
        *stats,
        scratch=[pltpu.VMEM((reps, rows, size), f32)],
    )
    update = call(
        lambda *refs: update_kernel(count, *refs),
        jax.ShapeDtypeStruct((1, rows, size), bf16),
        [SMEM] + [VMEM] * (ACROSS + 1),
        (2 * rows * size * size, 4 * size * size),
        place,
        root,
        *totals,
        scratch=[pltpu.VMEM((reps, rows, size), f32)],
    )
    new_state = call(
        state_kernel,
        shape(capacity, rows, size),
        [SMEM, VMEM, VMEM, ANY],
        (0, 4 * size * rows * 8),
        stat_source,
        held,
        returned,
        root,
    )
    return (new_state[None], update)


def solution(mesh):
    placed = (P("rep", "pre", None, None), P(), P("pre", None, "rep", None))
    return jax.shard_map(
        body,
        mesh=mesh,
        in_specs=placed,
        out_specs=(P("pre", None, "rep", None), P("pre", "rep", None)),
        check_vma=False,
    )
```

```python
import functools

import jax
import jax.numpy as jnp
from jax import lax
from jax.experimental import pallas as pl
from jax.experimental.pallas import tpu as pltpu
from jax.sharding import PartitionSpec as P

ITERS = 4
DAMP = 0.05
GROUP = 4
LANES = 128
ENTRY = 3
RETURN = 8 * ENTRY
ACROSS = 4
f32 = jnp.float32
bf16 = jnp.bfloat16

VMEM = pl.BlockSpec(memory_space=pltpu.VMEM)
ANY = pl.BlockSpec(memory_space=pl.ANY)
HBM = pl.BlockSpec(memory_space=pltpu.HBM)
SMEM = pl.BlockSpec(memory_space=pltpu.SMEM)
PARAMS = pltpu.CompilerParams(vmem_limit_bytes=40 * 2**20)


def call(kernel, out_shape, in_specs, cost, *args, scratch=(), out_specs=VMEM):
    multiple = isinstance(out_shape, (list, tuple))
    return pl.pallas_call(
        kernel,
        out_shape=out_shape,
        in_specs=in_specs,
        out_specs=[out_specs] * len(out_shape) if multiple else out_specs,
        scratch_shapes=list(scratch),
        compiler_params=PARAMS,
        cost_estimate=pl.CostEstimate(flops=cost[0], bytes_accessed=cost[1], transcendentals=0),
    )(*args)


def gram_kernel(grads_ref, out_ref):
    shards, size, _ = grads_ref.shape
    xs, zs, double, _ = out_ref.shape
    rows = double // 2
    gram = None
    total = None
    for s in range(shards):
        g = grads_ref[s]
        term = lax.dot_general(g, g, (((1,), (1,)), ((), ())), preferred_element_type=f32)
        gram = term if gram is None else gram + term
        wide = g.astype(f32)
        total = wide if total is None else total + wide
    gram = gram.reshape(zs, xs, rows, size)
    total = total.reshape(zs, xs, rows, size)
    for x in range(xs):
        out_ref[x, :, :rows, :] = gram[:, x]
        out_ref[x, :, rows:, :] = total[:, x]


def sum_kernel(parts_ref, after_ref, out_ref):
    del after_ref
    out_ref[...] = jnp.sum(parts_ref[...], axis=0)


def choose(k, options):
    value = options[0]
    for i in range(1, len(options)):
        value = jnp.where(k == i, options[i], value)
    return value


def table_kernel(me_ref, owner_ref, out_ref, count_ref, slot_ref, block_ref):
    blocks = owner_ref.shape[0]
    me = me_ref[0]
    y, q = me >> 2, me & 3
    for b in range(blocks):
        count_ref[b] = 0
    for i in range(9):
        block_ref[i] = -1
    for b in range(blocks):
        o = owner_ref[b]
        s = jnp.minimum(count_ref[o], 1)
        count_ref[o] = s + 1
        slot_ref[b] = s
        near = o ^ me
        block_ref[jnp.where(near < 4, near * 2 + s, 8)] = b

    def put(i, block, line, last=False):
        o = owner_ref[block]
        d = ((o ^ me) >> 2) & 3
        which = jnp.where(d == 0, (((o ^ q) >> 1) & 1) + 2 * ((o ^ q) & 1), 3 + d)
        if last:
            which = jnp.where((o >> 4) == (me >> 4), which, 7)
        out_ref[i * ENTRY] = which
        out_ref[i * ENTRY + 1] = slot_ref[block]
        out_ref[i * ENTRY + 2] = line

    for n in range(1, 4):
        for t in range(2):
            put((n - 1) * 2 + t, (((y & 3) ^ n) + 4 * t) * GROUP + q, t)
    put(6, me ^ 16, (me >> 4) ^ 1)
    put(7, me, me >> 4, True)
    for i in range(8):
        block = block_ref[i]
        out_ref[RETURN + 4 * i] = ((block ^ me) >> 2) & 3
        out_ref[RETURN + 4 * i + 1] = ((block ^ me) >> 4) & 1
        out_ref[RETURN + 4 * i + 2] = (block ^ me) & 1
        out_ref[RETURN + 4 * i + 3] = jnp.where(block < 0, 0, 1 + (((block ^ me) >> 1) & 1))


def columns(place, rows, size):
    first = place * rows // LANES
    return [pl.multiple_of((first + n) % (size // LANES) * LANES, LANES) for n in range(size // LANES - 1)]


def keep_kernel(place_ref, held_ref, held_z_ref, kept_ref):
    capacity, rows, size = held_ref.shape
    for n, column in enumerate(columns(place_ref[0], rows, size)):
        for i, held in enumerate((held_ref, held_z_ref)):
            for j in range(capacity):
                kept_ref[i, j, :, n * LANES : (n + 1) * LANES] = held[j, :, pl.ds(column, LANES)]


def pick(table_ref, entry, kept_ref, core_ref, near=(), far=()):
    which, slot, line = (table_ref[entry * ENTRY + i] for i in range(ENTRY))
    options = [k[i, slot] for k in (kept_ref, core_ref) for i in range(2)]
    return choose(which, options + [g[line] for g in near] + [g[...] for g in far])


def near_kernel(table_ref, kept_ref, core_ref, *outs):
    for n, out in enumerate(outs):
        for t in range(2):
            out[t] = pick(table_ref, n * 2 + t, kept_ref, core_ref)


def far_kernel(table_ref, kept_ref, core_ref, near1, near2, near3, out_ref):
    out_ref[...] = pick(table_ref, 6, kept_ref, core_ref, (near1, near2, near3))


def stat_kernel(table_ref, place_ref, sums_ref, kept_ref, core_ref, *refs):
    wide_ref, gram_ref, both_ref = refs[4:]
    rows, size = gram_ref.shape
    sums = jnp.sum(sums_ref[...], axis=0)
    gram_ref[...] = sums[:rows]
    keep = size - LANES
    for n, column in enumerate(columns(place_ref[0], rows, size)):
        both_ref[:, n * LANES : (n + 1) * LANES] = gram_ref[:, pl.ds(column, LANES)]
    both_ref[:, :keep] += pick(table_ref, 7, kept_ref, core_ref, refs[:3], refs[3:4])
    both_ref[:, keep:] = sums[rows:]
    wide_ref[...] = jnp.broadcast_to(both_ref[...][None], wide_ref.shape)


def stack_kernel(*refs):
    for m, part in enumerate(refs[:-1]):
        refs[-1][m] = part[...]


def return_kernel(table_ref, *refs):
    lines, (own_ref, core_ref) = refs[:-2], refs[-2:]
    for i in range(8):
        n, line = table_ref[RETURN + 4 * i], table_ref[RETURN + 4 * i + 1]
        out_ref = core_ref if i // 2 % 2 else own_ref
        out_ref[i // 4, i % 2] = choose(n, [g[line] for g in lines])


def pass_kernel(table_ref, own_ref, core_ref, mine_ref, send_ref):
    for k, out in enumerate((mine_ref, send_ref)):
        for j in range(2):
            other = table_ref[RETURN + 4 * (4 * k + j) + 2]
            out[j] = jnp.where(other == 0, own_ref[k, j], core_ref[k, j])


def state_kernel(table_ref, state_ref, mine_ref, got_ref, after_ref, out_ref):
    del after_ref
    for j in range(2):
        way = table_ref[RETURN + 4 * j + 3]
        gram = jnp.where(way == 1, mine_ref[j], got_ref[j])
        out_ref[j] = state_ref[j] + jnp.where(way > 0, gram, 0.0)


def split(a):
    high = a.astype(bf16)
    return high, (a - high.astype(f32)).astype(bf16)


def product(a, b):
    (a_high, a_low), (b_high, b_low) = a, b
    dot = lambda x, y: jnp.dot(x, y, preferred_element_type=f32)
    return dot(a_high, b_high) + (dot(a_high, b_low) + dot(a_low, b_high))


def copies_kernel(part_ref, after_ref, out_ref, sems):
    del after_ref
    copies = [pltpu.make_async_copy(part_ref, out_ref.at[x], sems.at[x]) for x in range(out_ref.shape[0])]
    for copy in copies:
        copy.start()
    for copy in copies:
        copy.wait()


def newton_kernel(count, place_ref, all_ref, after_ref, out_ref, end_ref, stat_ref):
    del after_ref
    end_ref[...] = jnp.zeros_like(end_ref)
    xs, zs, rows, wide = all_ref.shape
    size = stat_ref.shape[1]
    blocks = size // LANES
    place = place_ref[0]
    for z in range(zs):
        for n in range(blocks - 1):
            j = (z + n) % blocks
            part = jnp.concatenate([all_ref[x, z, :, n * LANES : (n + 1) * LANES] for x in range(xs)], axis=0)
            stat_ref[z * LANES : (z + 1) * LANES, j * LANES : (j + 1) * LANES] = part
            if n == 1:
                stat_ref[j * LANES : (j + 1) * LANES, z * LANES : (z + 1) * LANES] = part.T
    stat = stat_ref[...]
    row_ids = lax.broadcasted_iota(jnp.int32, (size, size), 0)
    col_ids = lax.broadcasted_iota(jnp.int32, (size, size), 1)
    eye = (row_ids == col_ids).astype(f32)
    thin_rows = lax.broadcasted_iota(jnp.int32, (rows, size), 0) + place * rows
    thin_cols = lax.broadcasted_iota(jnp.int32, (rows, size), 1)
    thin_eye = (thin_rows == thin_cols).astype(f32)
    norm = jnp.sqrt(jnp.sum(stat * stat))
    damped = stat + (DAMP * norm) * eye
    scale = jnp.sqrt(jnp.sum(damped * damped))
    iterate = damped / scale
    mine = stat_ref[pl.ds(pl.multiple_of(place * rows, rows), rows), :]
    mine = (mine + (DAMP * norm) * thin_eye) / scale
    thin = 1.25 * thin_eye - 0.25 * mine
    parts_of = split(iterate)
    for _ in range(ITERS - 2):
        square = product(parts_of, parts_of)
        factor2 = split(1.5625 * eye - 0.625 * iterate + 0.0625 * square)
        iterate = product(parts_of, split(product(factor2, factor2)))
        parts_of = split(iterate)
        thin = 1.25 * thin - 0.25 * product(split(thin), parts_of)
    last = product(split(thin), parts_of)
    for _ in range(4):
        last = 1.25 * last - 0.25 * product(split(last), parts_of)
    thin = (1.25 * thin - 0.25 * last) * jnp.exp(-0.25 * jnp.log(scale))
    mean = jnp.concatenate([all_ref[x, z, :, size - LANES :] for z in range(zs) for x in range(xs)], axis=0)
    mean = (mean / count).astype(bf16)
    out_ref[0] = jnp.dot(thin.astype(bf16), mean, preferred_element_type=f32).astype(bf16)


def body(grads, owner, state):
    local = grads[:, 0]
    shards, size, _ = local.shape
    held = state[0]
    capacity, rows, _ = held.shape
    reps = lax.axis_size("rep")
    blocks = owner.shape[0]
    groups = blocks // GROUP
    shape = lambda *s: jax.ShapeDtypeStruct(s, f32)

    def across(x, k):
        return lax.ppermute(x, "pre", [(i, i ^ k) for i in range(blocks)])

    zs = reps // ACROSS
    x_groups = [[z * ACROSS + x for x in range(ACROSS)] for z in range(zs)]
    z_groups = [[z * ACROSS + x for z in range(zs)] for x in range(ACROSS)]

    def exchange(x, which):
        return lax.all_to_all(x, "rep", 0, 0, tiled=True, axis_index_groups=which)

    me = lax.axis_index("pre").reshape(1).astype(jnp.int32)
    place = lax.axis_index("rep").reshape(1).astype(jnp.int32)
    table = pl.pallas_call(
        table_kernel,
        out_shape=jax.ShapeDtypeStruct((RETURN + 32,), jnp.int32),
        in_specs=[SMEM, SMEM],
        out_specs=SMEM,
        scratch_shapes=[
            pltpu.SMEM((blocks,), jnp.int32),
            pltpu.SMEM((blocks,), jnp.int32),
            pltpu.SMEM((16,), jnp.int32),
        ],
    )(me, owner)

    held_z = across(held, 2)
    sums = call(
        gram_kernel,
        shape(ACROSS, zs, 2 * rows, size),
        [VMEM],
        (2 * shards * size**3, 4 * size * size * (shards + 2)),
        local,
    )
    sums = exchange(sums, x_groups)
    kept = call(
        keep_kernel,
        shape(2, capacity, rows, size - LANES),
        [SMEM, VMEM, VMEM],
        (0, 4 * size * rows * 8),
        place,
        held,
        held_z,
    )
    core = across(kept, 1)
    near = call(
        near_kernel,
        [shape(2, rows, size - LANES)] * 3,
        [SMEM, VMEM, VMEM],
        (0, 4 * size * rows * 12),
        table,
        kept,
        core,
    )
    near = [across(sent, GROUP * (n + 1)) for n, sent in enumerate(near)]
    far = call(
        far_kernel,
        shape(rows, size - LANES),
        [SMEM] + [VMEM] * 5,
        (0, 4 * size * rows * 12),
        table,
        kept,
        core,
        *near,
    )
    sums = call(
        sum_kernel,
        shape(zs, 2 * rows, size),
        [VMEM, ANY],
        (0, 4 * size * rows * 40),
        sums,
        far,
    )
    sums = exchange(sums, z_groups)
    far = across(far, 4 * GROUP)
    both, gram = call(
        stat_kernel,
        [shape(zs, rows, 2 * size - LANES), shape(rows, size)],
        [SMEM, SMEM] + [VMEM] * 7,
        (0, 4 * size * rows * 45),
        table,
        place,
        sums,
        kept,
        core,
        *near,
        far,
        scratch=[pltpu.VMEM((rows, 2 * size - LANES), f32)],
    )
    both = exchange(both, z_groups)
    line = call(
        stack_kernel,
        shape(2, rows, size),
        [VMEM] * 2,
        (0, 4 * size * rows * 4),
        gram,
        across(gram, 4 * GROUP),
    )
    lines = [line] + [across(line, GROUP * n) for n in range(1, 4)]
    both = call(
        copies_kernel,
        shape(ACROSS, zs, rows, 2 * size - LANES),
        [VMEM, ANY],
        (0, 4 * size * rows * 40),
        both,
        lines[1],
        out_specs=HBM,
        scratch=[pltpu.SemaphoreType.DMA((ACROSS,))],
    )
    both = exchange(both, x_groups)
    own, core = call(
        return_kernel,
        [shape(2, capacity, rows, size)] * 2,
        [SMEM] + [VMEM] * 4,
        (0, 4 * size * rows * 24),
        table,
        *lines,
    )
    mine, passed = call(
        pass_kernel,
        [shape(capacity, rows, size)] * 2,
        [SMEM, VMEM, VMEM],
        (0, 4 * size * rows * 12),
        table,
        own,
        across(core, 1),
    )
    count = shards * reps
    update, end = call(
        functools.partial(newton_kernel, count),
        [jax.ShapeDtypeStruct((1, rows, size), bf16), shape(8, LANES)],
        [SMEM, VMEM, ANY],
        (2 * 20 * size**3, 8 * size * size),
        place,
        both,
        passed,
        scratch=[pltpu.VMEM((size, size), f32)],
    )
    new_state = call(
        state_kernel,
        shape(capacity, rows, size),
        [SMEM, VMEM, VMEM, VMEM, ANY],
        (0, 4 * size * rows * 8),
        table,
        held,
        mine,
        across(passed, 2),
        end,
    )
    return (new_state[None], update)


def solution(mesh):
    placed = (P("rep", "pre", None, None), P(), P("pre", None, "rep", None))
    return jax.shard_map(
        body,
        mesh=mesh,
        in_specs=placed,
        out_specs=(P("pre", None, "rep", None), P("pre", "rep", None)),
        check_vma=False,
    )
```

```python
import functools

import jax
import jax.numpy as jnp
from jax import lax
from jax.experimental import pallas as pl
from jax.experimental.pallas import tpu as pltpu
from jax.sharding import PartitionSpec as P

ITERS = 4
DAMP = 0.05
GROUP = 4
LANES = 128
ENTRY = 3
RETURN = 8 * ENTRY
ACROSS = 4
f32 = jnp.float32
bf16 = jnp.bfloat16

VMEM = pl.BlockSpec(memory_space=pltpu.VMEM)
ANY = pl.BlockSpec(memory_space=pl.ANY)
HBM = pl.BlockSpec(memory_space=pltpu.HBM)
SMEM = pl.BlockSpec(memory_space=pltpu.SMEM)


def call(kernel, out_shape, in_specs, cost, *args, scratch=(), out_specs=VMEM, limit=40):
    multiple = isinstance(out_shape, (list, tuple))
    return pl.pallas_call(
        kernel,
        out_shape=out_shape,
        in_specs=in_specs,
        out_specs=[out_specs] * len(out_shape) if multiple else out_specs,
        scratch_shapes=list(scratch),
        compiler_params=pltpu.CompilerParams(vmem_limit_bytes=limit * 2**20),
        cost_estimate=pl.CostEstimate(flops=cost[0], bytes_accessed=cost[1], transcendentals=0),
    )(*args)


def gram_kernel(grads_hbm, out_ref, grads_ref, whole_ref, in_sems, out_sems):
    shards, size, _ = grads_ref.shape
    xs, zs, double, _ = out_ref.shape
    rows = double // 2
    loads = [pltpu.make_async_copy(grads_hbm.at[s], grads_ref.at[s], in_sems.at[s]) for s in range(shards)]
    for load in loads:
        load.start()
    for load in loads:
        load.wait()
    stores = []
    half = size // 2
    for h in range(2):
        gram = None
        total = None
        for s in range(shards):
            mine = grads_ref[s, h * half : (h + 1) * half]
            term = lax.dot_general(mine, grads_ref[s], (((1,), (1,)), ((), ())), preferred_element_type=f32)
            gram = term if gram is None else gram + term
            wide = mine.astype(f32)
            total = wide if total is None else total + wide
        gram = gram.reshape(zs // 2, xs, rows, size)
        total = total.reshape(zs // 2, xs, rows, size)
        part = slice(h * zs // 2, (h + 1) * zs // 2)
        for x in range(xs):
            whole_ref[x, part, :rows, :] = gram[:, x]
            whole_ref[x, part, rows:, :] = total[:, x]
            stores.append(pltpu.make_async_copy(whole_ref.at[x, part], out_ref.at[x, part], out_sems.at[h, x]))
            stores[-1].start()
    for store in stores:
        store.wait()


def sum_kernel(parts_ref, after_ref, out_ref):
    del after_ref
    out_ref[...] = jnp.sum(parts_ref[...], axis=0)


def choose(k, options):
    value = options[0]
    for i in range(1, len(options)):
        value = jnp.where(k == i, options[i], value)
    return value


def table_kernel(me_ref, owner_ref, out_ref, count_ref, slot_ref, block_ref):
    blocks = owner_ref.shape[0]
    me = me_ref[0]
    y, q = me >> 2, me & 3
    for b in range(blocks):
        count_ref[b] = 0
    for i in range(9):
        block_ref[i] = -1
    for b in range(blocks):
        o = owner_ref[b]
        s = jnp.minimum(count_ref[o], 1)
        count_ref[o] = s + 1
        slot_ref[b] = s
        near = o ^ me
        block_ref[jnp.where(near < 4, near * 2 + s, 8)] = b

    def put(i, block, line, last=False):
        o = owner_ref[block]
        d = ((o ^ me) >> 2) & 3
        which = jnp.where(d == 0, (((o ^ q) >> 1) & 1) + 2 * ((o ^ q) & 1), 3 + d)
        if last:
            which = jnp.where((o >> 4) == (me >> 4), which, 7)
        out_ref[i * ENTRY] = which
        out_ref[i * ENTRY + 1] = slot_ref[block]
        out_ref[i * ENTRY + 2] = line

    for n in range(1, 4):
        for t in range(2):
            put((n - 1) * 2 + t, (((y & 3) ^ n) + 4 * t) * GROUP + q, t)
    put(6, me ^ 16, (me >> 4) ^ 1)
    put(7, me, me >> 4, True)
    for i in range(8):
        block = block_ref[i]
        out_ref[RETURN + 3 * i] = ((block ^ me) >> 2) & 1
        out_ref[RETURN + 3 * i + 1] = (((block ^ me) >> 4) & 1) + 2 * (((block ^ me) >> 3) & 1)
        out_ref[RETURN + 3 * i + 2] = jnp.where(block < 0, -1, (block ^ me) & 3)


def columns(place, rows, size):
    first = place * rows // LANES
    return [pl.multiple_of((first + n) % (size // LANES) * LANES, LANES) for n in range(size // LANES - 1)]


def keep_kernel(place_ref, held_ref, held_z_ref, kept_ref):
    capacity, rows, size = held_ref.shape
    for n, column in enumerate(columns(place_ref[0], rows, size)):
        for i, held in enumerate((held_ref, held_z_ref)):
            for j in range(capacity):
                kept_ref[i, j, :, n * LANES : (n + 1) * LANES] = held[j, :, pl.ds(column, LANES)]


def pick(table_ref, entry, kept_ref, core_ref, near=(), far=()):
    which, slot, line = (table_ref[entry * ENTRY + i] for i in range(ENTRY))
    options = [k[i, slot] for k in (kept_ref, core_ref) for i in range(2)]
    return choose(which, options + [g[line] for g in near] + [g[...] for g in far])


def near_kernel(table_ref, kept_ref, core_ref, *outs):
    for n, out in enumerate(outs):
        for t in range(2):
            out[t] = pick(table_ref, n * 2 + t, kept_ref, core_ref)


def far_kernel(table_ref, kept_ref, core_ref, near1, near2, near3, out_ref):
    out_ref[...] = pick(table_ref, 6, kept_ref, core_ref, (near1, near2, near3))


def stat_kernel(table_ref, place_ref, sums_ref, kept_ref, core_ref, *refs):
    wide_ref, gram_ref, both_ref = refs[4:]
    _, rows, size = gram_ref.shape
    sums = jnp.sum(sums_ref[...], axis=0)
    gram_ref[0] = sums[:rows]
    keep = size - LANES
    for n, column in enumerate(columns(place_ref[0], rows, size)):
        both_ref[:, n * LANES : (n + 1) * LANES] = gram_ref[0, :, pl.ds(column, LANES)]
    both_ref[:, :keep] += pick(table_ref, 7, kept_ref, core_ref, refs[:3], refs[3:4])
    both_ref[:, keep:] = sums[rows:]
    wide_ref[...] = jnp.broadcast_to(both_ref[...][None], wide_ref.shape)


def stack_kernel(first_ref, second_ref, out_ref):
    half = out_ref.shape[0] // 2
    out_ref[:half] = first_ref[...]
    out_ref[half:] = second_ref[...]


def return_kernel(table_ref, line_ref, far_ref, *outs):
    for i in range(8):
        n, line = table_ref[RETURN + 3 * i], table_ref[RETURN + 3 * i + 1]
        outs[i // 2][i % 2] = choose(n, [line_ref[line], far_ref[line]])


def state_kernel(table_ref, state_ref, got0, got1, got2, got3, after_ref, out_ref):
    del after_ref
    for j in range(2):
        way = table_ref[RETURN + 3 * j + 2]
        gram = choose(way, [got0[j], got1[j], got2[j], got3[j]])
        out_ref[j] = state_ref[j] + jnp.where(way >= 0, gram, 0.0)


def split(a):
    high = a.astype(bf16)
    return high, (a - high.astype(f32)).astype(bf16)


def product(a, b):
    (a_high, a_low), (b_high, b_low) = a, b
    return jnp.dot(
        jnp.concatenate([a_high, a_high, a_low], axis=1),
        jnp.concatenate([b_high, b_low, b_high], axis=0),
        preferred_element_type=f32,
    )


def copies_kernel(part_ref, after_ref, out_ref, sems):
    del after_ref
    copies = [pltpu.make_async_copy(part_ref, out_ref.at[x], sems.at[x]) for x in range(out_ref.shape[0])]
    for copy in copies:
        copy.start()
    for copy in copies:
        copy.wait()


def thin_product(a, b):
    a_high, a_low = split(a)
    rows = a.shape[0]
    both = jnp.dot(jnp.concatenate([a_high, a_low], axis=0), b[0], preferred_element_type=f32)
    return both[:rows] + (both[rows:] + jnp.dot(a_high, b[1], preferred_element_type=f32))


def newton_kernel(count, place_ref, all_ref, after_ref, out_ref, end_ref, stat_ref):
    del after_ref
    end_ref[...] = jnp.zeros_like(end_ref)
    xs, zs, rows, wide = all_ref.shape
    size = stat_ref.shape[1]
    blocks = size // LANES
    place = place_ref[0]
    for z in range(zs):
        for n in range(blocks - 1):
            j = (z + n) % blocks
            part = jnp.concatenate([all_ref[x, z, :, n * LANES : (n + 1) * LANES] for x in range(xs)], axis=0)
            stat_ref[z * LANES : (z + 1) * LANES, j * LANES : (j + 1) * LANES] = part
            if n == 1:
                stat_ref[j * LANES : (j + 1) * LANES, z * LANES : (z + 1) * LANES] = part.T
    stat = stat_ref[...]
    diagonal = lax.broadcasted_iota(jnp.int32, (size, size), 0) == lax.broadcasted_iota(jnp.int32, (size, size), 1)
    plus = lambda a, m: jnp.where(diagonal, m + a, m)
    thin_rows = lax.broadcasted_iota(jnp.int32, (rows, size), 0) + place * rows
    thin_cols = lax.broadcasted_iota(jnp.int32, (rows, size), 1)
    thin_eye = (thin_rows == thin_cols).astype(f32)
    norm = jnp.sqrt(jnp.sum(stat * stat))
    damped = plus(DAMP * norm, stat)
    scale = jnp.sqrt(jnp.sum(damped * damped))
    iterate = damped / scale
    mine = stat_ref[pl.ds(pl.multiple_of(place * rows, rows), rows), :]
    mine = (mine + (DAMP * norm) * thin_eye) / scale
    thin = 1.25 * thin_eye - 0.25 * mine
    parts_of = split(iterate)
    for _ in range(ITERS - 2):
        square = product(parts_of, parts_of)
        factor2 = split(plus(1.5625, 0.0625 * square - 0.625 * iterate))
        iterate = product(parts_of, split(product(factor2, factor2)))
        parts_of = split(iterate)
        thin = 1.25 * thin - 0.25 * thin_product(thin, parts_of)
    last = thin_product(thin, parts_of)
    for _ in range(4):
        last = 1.25 * last - 0.25 * thin_product(last, parts_of)
    thin = (1.25 * thin - 0.25 * last) * jnp.exp(-0.25 * jnp.log(scale))
    mean = jnp.concatenate([all_ref[x, z, :, size - LANES :] for z in range(zs) for x in range(xs)], axis=0)
    mean = (mean / count).astype(bf16)
    out_ref[0] = jnp.dot(thin.astype(bf16), mean, preferred_element_type=f32).astype(bf16)


def body(grads, owner, state):
    local = grads[:, 0]
    shards, size, _ = local.shape
    held = state[0]
    capacity, rows, _ = held.shape
    reps = lax.axis_size("rep")
    blocks = owner.shape[0]
    groups = blocks // GROUP
    shape = lambda *s: jax.ShapeDtypeStruct(s, f32)

    def across(x, k):
        return lax.ppermute(x, "pre", [(i, i ^ k) for i in range(blocks)])

    zs = reps // ACROSS
    x_groups = [[z * ACROSS + x for x in range(ACROSS)] for z in range(zs)]
    z_groups = [[z * ACROSS + x for z in range(zs)] for x in range(ACROSS)]

    def exchange(x, which):
        return lax.all_to_all(x, "rep", 0, 0, tiled=True, axis_index_groups=which)

    me = lax.axis_index("pre").reshape(1).astype(jnp.int32)
    place = lax.axis_index("rep").reshape(1).astype(jnp.int32)
    table = pl.pallas_call(
        table_kernel,
        out_shape=jax.ShapeDtypeStruct((RETURN + 24,), jnp.int32),
        in_specs=[SMEM, SMEM],
        out_specs=SMEM,
        scratch_shapes=[
            pltpu.SMEM((blocks,), jnp.int32),
            pltpu.SMEM((blocks,), jnp.int32),
            pltpu.SMEM((16,), jnp.int32),
        ],
    )(me, owner)

    held_z = across(held, 2)
    sums = call(
        gram_kernel,
        shape(ACROSS, zs, 2 * rows, size),
        [ANY],
        (2 * shards * size**3, 4 * size * size * (shards + 2)),
        local,
        limit=60,
        out_specs=ANY,
        scratch=[
            pltpu.VMEM(local.shape, local.dtype),
            pltpu.VMEM((ACROSS, zs, 2 * rows, size), f32),
            pltpu.SemaphoreType.DMA((shards,)),
            pltpu.SemaphoreType.DMA((2, ACROSS)),
        ],
    )
    sums = exchange(sums, x_groups)
    kept = call(
        keep_kernel,
        shape(2, capacity, rows, size - LANES),
        [SMEM, VMEM, VMEM],
        (2 * 100 * size**3, 4 * size * rows * 8),
        place,
        held,
        held_z,
    )
    core = across(kept, 1)
    near = call(
        near_kernel,
        [shape(2, rows, size - LANES)] * 3,
        [SMEM, VMEM, VMEM],
        (0, 4 * size * rows * 12),
        table,
        kept,
        core,
    )
    near = [across(sent, GROUP * (n + 1)) for n, sent in enumerate(near)]
    far = call(
        far_kernel,
        shape(rows, size - LANES),
        [SMEM] + [VMEM] * 5,
        (0, 4 * size * rows * 12),
        table,
        kept,
        core,
        *near,
    )
    sums = call(
        sum_kernel,
        shape(zs, 2 * rows, size),
        [VMEM, ANY],
        (0, 4 * size * rows * 40),
        sums,
        far,
    )
    sums = exchange(sums, z_groups)
    far = across(far, 4 * GROUP)
    both, gram = call(
        stat_kernel,
        [shape(zs, rows, 2 * size - LANES), shape(1, rows, size)],
        [SMEM, SMEM] + [VMEM] * 7,
        (0, 4 * size * rows * 45),
        table,
        place,
        sums,
        kept,
        core,
        *near,
        far,
        scratch=[pltpu.VMEM((rows, 2 * size - LANES), f32)],
    )
    both = exchange(both, z_groups)
    line = gram
    lines = []
    for bit in (4, 2):
        line = call(
            stack_kernel,
            shape(2 * line.shape[0], rows, size),
            [VMEM] * 2,
            (0, 4 * size * rows * 8),
            line,
            across(line, GROUP * bit),
        )
        lines.append(line)
    both = call(
        copies_kernel,
        shape(ACROSS, zs, rows, 2 * size - LANES),
        [VMEM, ANY],
        (0, 4 * size * rows * 40),
        both,
        lines[0],
        out_specs=HBM,
        scratch=[pltpu.SemaphoreType.DMA((ACROSS,))],
    )
    both = exchange(both, x_groups)
    own, *sent = call(
        return_kernel,
        [shape(capacity, rows, size)] * 4,
        [SMEM] + [VMEM] * 2,
        (0, 4 * size * rows * 24),
        table,
        line,
        across(line, GROUP),
    )
    count = shards * reps
    update, end = call(
        functools.partial(newton_kernel, count),
        [jax.ShapeDtypeStruct((1, rows, size), bf16), shape(8, LANES)],
        [SMEM, VMEM, ANY],
        (2 * 20 * size**3, 8 * size * size),
        place,
        both,
        own,
        scratch=[pltpu.VMEM((size, size), f32)],
    )
    new_state = call(
        state_kernel,
        shape(capacity, rows, size),
        [SMEM] + [VMEM] * 5 + [ANY],
        (0, 4 * size * rows * 8),
        table,
        held,
        own,
        *[across(rows_sent, k + 1) for k, rows_sent in enumerate(sent)],
        end,
    )
    return (new_state[None], update)


def solution(mesh):
    placed = (P("rep", "pre", None, None), P(), P("pre", None, "rep", None))
    return jax.shard_map(
        body,
        mesh=mesh,
        in_specs=placed,
        out_specs=(P("pre", None, "rep", None), P("pre", "rep", None)),
        check_vma=False,
    )
```

```python
import functools

import jax
import jax.numpy as jnp
from jax import lax
from jax.experimental import pallas as pl
from jax.experimental.pallas import tpu as pltpu
from jax.sharding import PartitionSpec as P

ITERS = 4
DAMP = 0.05
GROUP = 4
LANES = 128
ENTRY = 3
RETURN = 8 * ENTRY
ACROSS = 4
f32 = jnp.float32
bf16 = jnp.bfloat16

VMEM = pl.BlockSpec(memory_space=pltpu.VMEM)
ANY = pl.BlockSpec(memory_space=pl.ANY)
HBM = pl.BlockSpec(memory_space=pltpu.HBM)
SMEM = pl.BlockSpec(memory_space=pltpu.SMEM)


def call(kernel, out_shape, in_specs, cost, *args, scratch=(), out_specs=VMEM, limit=40):
    multiple = isinstance(out_shape, (list, tuple))
    return pl.pallas_call(
        kernel,
        out_shape=out_shape,
        in_specs=in_specs,
        out_specs=[out_specs] * len(out_shape) if multiple else out_specs,
        scratch_shapes=list(scratch),
        compiler_params=pltpu.CompilerParams(vmem_limit_bytes=limit * 2**20),
        cost_estimate=pl.CostEstimate(flops=cost[0], bytes_accessed=cost[1], transcendentals=0),
    )(*args)


def gram_kernel(grads_hbm, out_ref, grads_ref, whole_ref, in_sems, out_sems):
    shards, size, _ = grads_ref.shape
    xs, zs, double, _ = out_ref.shape
    rows = double // 2
    loads = [pltpu.make_async_copy(grads_hbm.at[s], grads_ref.at[s], in_sems.at[s]) for s in range(shards)]
    for load in loads:
        load.start()
    for load in loads:
        load.wait()
    stores = []
    half = size // 2
    for h in range(2):
        gram = None
        total = None
        for s in range(shards):
            mine = grads_ref[s, h * half : (h + 1) * half]
            term = lax.dot_general(mine, grads_ref[s], (((1,), (1,)), ((), ())), preferred_element_type=f32)
            gram = term if gram is None else gram + term
            wide = mine.astype(f32)
            total = wide if total is None else total + wide
        gram = gram.reshape(zs // 2, xs, rows, size)
        total = total.reshape(zs // 2, xs, rows, size)
        part = slice(h * zs // 2, (h + 1) * zs // 2)
        for x in range(xs):
            whole_ref[x, part, :rows, :] = gram[:, x]
            whole_ref[x, part, rows:, :] = total[:, x]
            stores.append(pltpu.make_async_copy(whole_ref.at[x, part], out_ref.at[x, part], out_sems.at[h, x]))
            stores[-1].start()
    for store in stores:
        store.wait()


def sum_kernel(parts_ref, after_ref, out_ref):
    del after_ref
    out_ref[...] = jnp.sum(parts_ref[...], axis=0)


def choose(k, options):
    value = options[0]
    for i in range(1, len(options)):
        value = jnp.where(k == i, options[i], value)
    return value


def table_kernel(me_ref, owner_ref, out_ref, count_ref, slot_ref, block_ref):
    blocks = owner_ref.shape[0]
    me = me_ref[0]
    y, q = me >> 2, me & 3
    for b in range(blocks):
        count_ref[b] = 0
    for i in range(9):
        block_ref[i] = -1
    for b in range(blocks):
        o = owner_ref[b]
        s = jnp.minimum(count_ref[o], 1)
        count_ref[o] = s + 1
        slot_ref[b] = s
        near = o ^ me
        block_ref[jnp.where(near < 4, near * 2 + s, 8)] = b

    def put(i, block, line, last=False):
        o = owner_ref[block]
        d = ((o ^ me) >> 2) & 3
        which = jnp.where(d == 0, (((o ^ q) >> 1) & 1) + 2 * ((o ^ q) & 1), 3 + d)
        if last:
            which = jnp.where((o >> 4) == (me >> 4), which, 7)
        out_ref[i * ENTRY] = which
        out_ref[i * ENTRY + 1] = slot_ref[block]
        out_ref[i * ENTRY + 2] = line

    for n in range(1, 4):
        for t in range(2):
            put((n - 1) * 2 + t, (((y & 3) ^ n) + 4 * t) * GROUP + q, t)
    put(6, me ^ 16, (me >> 4) ^ 1)
    put(7, me, me >> 4, True)
    for i in range(8):
        block = block_ref[i]
        out_ref[RETURN + 3 * i] = ((block ^ me) >> 2) & 1
        out_ref[RETURN + 3 * i + 1] = (((block ^ me) >> 4) & 1) + 2 * (((block ^ me) >> 3) & 1)
        out_ref[RETURN + 3 * i + 2] = jnp.where(block < 0, -1, (block ^ me) & 3)


def columns(place, rows, size):
    first = place * rows // LANES
    return [pl.multiple_of((first + n) % (size // LANES) * LANES, LANES) for n in range(size // LANES - 1)]


def keep_kernel(place_ref, held_ref, held_z_ref, kept_ref):
    capacity, rows, size = held_ref.shape
    for n, column in enumerate(columns(place_ref[0], rows, size)):
        for i, held in enumerate((held_ref, held_z_ref)):
            for j in range(capacity):
                kept_ref[i, j, :, n * LANES : (n + 1) * LANES] = held[j, :, pl.ds(column, LANES)]


def pick(table_ref, entry, kept_ref, core_ref, near=(), far=()):
    which, slot, line = (table_ref[entry * ENTRY + i] for i in range(ENTRY))
    options = [k[i, slot] for k in (kept_ref, core_ref) for i in range(2)]
    return choose(which, options + [g[line] for g in near] + [g[...] for g in far])


def near_kernel(table_ref, kept_ref, core_ref, *outs):
    for n, out in enumerate(outs):
        for t in range(2):
            out[t] = pick(table_ref, n * 2 + t, kept_ref, core_ref)


def far_kernel(table_ref, kept_ref, core_ref, near1, near2, near3, out_ref):
    out_ref[...] = pick(table_ref, 6, kept_ref, core_ref, (near1, near2, near3))


def stat_kernel(table_ref, place_ref, sums_ref, kept_ref, core_ref, *refs):
    wide_ref, gram_ref, both_ref = refs[4:]
    _, rows, size = gram_ref.shape
    sums = jnp.sum(sums_ref[...], axis=0)
    gram_ref[0] = sums[:rows]
    keep = size - LANES
    for n, column in enumerate(columns(place_ref[0], rows, size)):
        both_ref[:, n * LANES : (n + 1) * LANES] = gram_ref[0, :, pl.ds(column, LANES)]
    both_ref[:, :keep] += pick(table_ref, 7, kept_ref, core_ref, refs[:3], refs[3:4])
    both_ref[:, keep:] = sums[rows:]
    wide_ref[...] = jnp.broadcast_to(both_ref[...][None], wide_ref.shape)


def stack_kernel(first_ref, second_ref, out_ref):
    half = out_ref.shape[0] // 2
    out_ref[:half] = first_ref[...]
    out_ref[half:] = second_ref[...]


def return_kernel(table_ref, line_ref, far_ref, *outs):
    for i in range(8):
        n, line = table_ref[RETURN + 3 * i], table_ref[RETURN + 3 * i + 1]
        outs[i // 2][i % 2] = choose(n, [line_ref[line], far_ref[line]])


def state_kernel(table_ref, state_ref, got0, got1, got2, got3, after_ref, out_ref):
    del after_ref
    for j in range(2):
        way = table_ref[RETURN + 3 * j + 2]
        gram = choose(way, [got0[j], got1[j], got2[j], got3[j]])
        out_ref[j] = state_ref[j] + jnp.where(way >= 0, gram, 0.0)


def split(a):
    high = a.astype(bf16)
    return high, (a - high.astype(f32)).astype(bf16)


def product(a, b):
    (a_high, a_low), (b_high, b_low) = a, b
    half = a_high.shape[0] // 2
    left = jnp.concatenate([a_high, a_high, a_low], axis=1)
    right = jnp.concatenate([b_high, b_low, b_high], axis=0)
    top = jnp.dot(left[:half], right, preferred_element_type=f32)
    corner = jnp.dot(left[half:], right[:, half:], preferred_element_type=f32)
    return jnp.concatenate([top, jnp.concatenate([top[:, half:].T, corner], axis=1)], axis=0)


def copies_kernel(part_ref, after_ref, out_ref, sems):
    del after_ref
    copies = [pltpu.make_async_copy(part_ref, out_ref.at[x], sems.at[x]) for x in range(out_ref.shape[0])]
    for copy in copies:
        copy.start()
    for copy in copies:
        copy.wait()


def thin_product(a, b):
    a_high, a_low = split(a)
    rows = a.shape[0]
    both = jnp.dot(jnp.concatenate([a_high, a_low], axis=0), b[0], preferred_element_type=f32)
    return both[:rows] + (both[rows:] + jnp.dot(a_high, b[1], preferred_element_type=f32))


def newton_kernel(count, place_ref, all_ref, after_ref, out_ref, end_ref, stat_ref):
    del after_ref
    end_ref[...] = jnp.zeros_like(end_ref)
    xs, zs, rows, wide = all_ref.shape
    size = stat_ref.shape[1]
    blocks = size // LANES
    place = place_ref[0]
    for z in range(zs):
        for n in range(blocks - 1):
            j = (z + n) % blocks
            part = jnp.concatenate([all_ref[x, z, :, n * LANES : (n + 1) * LANES] for x in range(xs)], axis=0)
            stat_ref[z * LANES : (z + 1) * LANES, j * LANES : (j + 1) * LANES] = part
            if n == 1:
                stat_ref[j * LANES : (j + 1) * LANES, z * LANES : (z + 1) * LANES] = part.T
    stat = stat_ref[...]
    diagonal = lax.broadcasted_iota(jnp.int32, (size, size), 0) == lax.broadcasted_iota(jnp.int32, (size, size), 1)
    plus = lambda a, m: jnp.where(diagonal, m + a, m)
    thin_rows = lax.broadcasted_iota(jnp.int32, (rows, size), 0) + place * rows
    thin_cols = lax.broadcasted_iota(jnp.int32, (rows, size), 1)
    thin_eye = (thin_rows == thin_cols).astype(f32)
    norm = jnp.sqrt(jnp.sum(stat * stat))
    damped = plus(DAMP * norm, stat)
    scale = jnp.sqrt(jnp.sum(damped * damped))
    iterate = damped / scale
    mine = stat_ref[pl.ds(pl.multiple_of(place * rows, rows), rows), :]
    mine = (mine + (DAMP * norm) * thin_eye) / scale
    thin = 1.25 * thin_eye - 0.25 * mine
    parts_of = split(iterate)
    for _ in range(ITERS - 2):
        square = product(parts_of, parts_of)
        factor2 = split(plus(1.5625, 0.0625 * square - 0.625 * iterate))
        iterate = product(parts_of, split(product(factor2, factor2)))
        parts_of = split(iterate)
        thin = 1.25 * thin - 0.25 * thin_product(thin, parts_of)
    last = thin_product(thin, parts_of)
    for _ in range(4):
        last = 1.25 * last - 0.25 * thin_product(last, parts_of)
    thin = (1.25 * thin - 0.25 * last) * jnp.exp(-0.25 * jnp.log(scale))
    mean = jnp.concatenate([all_ref[x, z, :, size - LANES :] for z in range(zs) for x in range(xs)], axis=0)
    mean = (mean / count).astype(bf16)
    out_ref[0] = jnp.dot(thin.astype(bf16), mean, preferred_element_type=f32).astype(bf16)


def body(grads, owner, state):
    local = grads[:, 0]
    shards, size, _ = local.shape
    held = state[0]
    capacity, rows, _ = held.shape
    reps = lax.axis_size("rep")
    blocks = owner.shape[0]
    groups = blocks // GROUP
    shape = lambda *s: jax.ShapeDtypeStruct(s, f32)

    def across(x, k):
        return lax.ppermute(x, "pre", [(i, i ^ k) for i in range(blocks)])

    zs = reps // ACROSS
    x_groups = [[z * ACROSS + x for x in range(ACROSS)] for z in range(zs)]
    z_groups = [[z * ACROSS + x for z in range(zs)] for x in range(ACROSS)]

    def exchange(x, which):
        return lax.all_to_all(x, "rep", 0, 0, tiled=True, axis_index_groups=which)

    me = lax.axis_index("pre").reshape(1).astype(jnp.int32)
    place = lax.axis_index("rep").reshape(1).astype(jnp.int32)
    table = pl.pallas_call(
        table_kernel,
        out_shape=jax.ShapeDtypeStruct((RETURN + 24,), jnp.int32),
        in_specs=[SMEM, SMEM],
        out_specs=SMEM,
        scratch_shapes=[
            pltpu.SMEM((blocks,), jnp.int32),
            pltpu.SMEM((blocks,), jnp.int32),
            pltpu.SMEM((16,), jnp.int32),
        ],
    )(me, owner)

    held_z = across(held, 2)
    sums = call(
        gram_kernel,
        shape(ACROSS, zs, 2 * rows, size),
        [ANY],
        (2 * shards * size**3, 4 * size * size * (shards + 2)),
        local,
        limit=60,
        out_specs=ANY,
        scratch=[
            pltpu.VMEM(local.shape, local.dtype),
            pltpu.VMEM((ACROSS, zs, 2 * rows, size), f32),
            pltpu.SemaphoreType.DMA((shards,)),
            pltpu.SemaphoreType.DMA((2, ACROSS)),
        ],
    )
    sums = exchange(sums, x_groups)
    kept = call(
        keep_kernel,
        shape(2, capacity, rows, size - LANES),
        [SMEM, VMEM, VMEM],
        (2 * 100 * size**3, 4 * size * rows * 8),
        place,
        held,
        held_z,
    )
    core = across(kept, 1)
    near = call(
        near_kernel,
        [shape(2, rows, size - LANES)] * 3,
        [SMEM, VMEM, VMEM],
        (0, 4 * size * rows * 12),
        table,
        kept,
        core,
    )
    near = [across(sent, GROUP * (n + 1)) for n, sent in enumerate(near)]
    far = call(
        far_kernel,
        shape(rows, size - LANES),
        [SMEM] + [VMEM] * 5,
        (0, 4 * size * rows * 12),
        table,
        kept,
        core,
        *near,
    )
    sums = call(
        sum_kernel,
        shape(zs, 2 * rows, size),
        [VMEM, ANY],
        (0, 4 * size * rows * 40),
        sums,
        far,
    )
    sums = exchange(sums, z_groups)
    far = across(far, 4 * GROUP)
    both, gram = call(
        stat_kernel,
        [shape(zs, rows, 2 * size - LANES), shape(1, rows, size)],
        [SMEM, SMEM] + [VMEM] * 7,
        (0, 4 * size * rows * 45),
        table,
        place,
        sums,
        kept,
        core,
        *near,
        far,
        scratch=[pltpu.VMEM((rows, 2 * size - LANES), f32)],
    )
    both = exchange(both, z_groups)
    line = gram
    lines = []
    for bit in (4, 2):
        line = call(
            stack_kernel,
            shape(2 * line.shape[0], rows, size),
            [VMEM] * 2,
            (2 * (60 if bit == 2 else 0) * size**3, 4 * size * rows * 8),
            line,
            across(line, GROUP * bit),
        )
        lines.append(line)
    both = call(
        copies_kernel,
        shape(ACROSS, zs, rows, 2 * size - LANES),
        [VMEM, ANY],
        (0, 4 * size * rows * 40),
        both,
        lines[0],
        out_specs=HBM,
        scratch=[pltpu.SemaphoreType.DMA((ACROSS,))],
    )
    both = exchange(both, x_groups)
    own, *sent = call(
        return_kernel,
        [shape(capacity, rows, size)] * 4,
        [SMEM] + [VMEM] * 2,
        (0, 4 * size * rows * 24),
        table,
        line,
        across(line, GROUP),
    )
    count = shards * reps
    update, end = call(
        functools.partial(newton_kernel, count),
        [jax.ShapeDtypeStruct((1, rows, size), bf16), shape(8, LANES)],
        [SMEM, VMEM, ANY],
        (2 * 20 * size**3, 8 * size * size),
        place,
        both,
        own,
        scratch=[pltpu.VMEM((size, size), f32)],
    )
    new_state = call(
        state_kernel,
        shape(capacity, rows, size),
        [SMEM] + [VMEM] * 5 + [ANY],
        (0, 4 * size * rows * 8),
        table,
        held,
        own,
        *[across(rows_sent, k + 1) for k, rows_sent in enumerate(sent)],
        end,
    )
    return (new_state[None], update)


def solution(mesh):
    placed = (P("rep", "pre", None, None), P(), P("pre", None, "rep", None))
    return jax.shard_map(
        body,
        mesh=mesh,
        in_specs=placed,
        out_specs=(P("pre", None, "rep", None), P("pre", "rep", None)),
        check_vma=False,
    )
```

```python
import functools

import jax
import jax.numpy as jnp
from jax import lax
from jax.experimental import pallas as pl
from jax.experimental.pallas import tpu as pltpu
from jax.sharding import PartitionSpec as P

ITERS = 4
DAMP = 0.05
GROUP = 4
LANES = 128
ENTRY = 3
RETURN = 8 * ENTRY
ACROSS = 4
f32 = jnp.float32
bf16 = jnp.bfloat16

VMEM = pl.BlockSpec(memory_space=pltpu.VMEM)
ANY = pl.BlockSpec(memory_space=pl.ANY)
HBM = pl.BlockSpec(memory_space=pltpu.HBM)
SMEM = pl.BlockSpec(memory_space=pltpu.SMEM)


def call(kernel, out_shape, in_specs, cost, *args, scratch=(), out_specs=VMEM, limit=40):
    multiple = isinstance(out_shape, (list, tuple))
    return pl.pallas_call(
        kernel,
        out_shape=out_shape,
        in_specs=in_specs,
        out_specs=[out_specs] * len(out_shape) if multiple else out_specs,
        scratch_shapes=list(scratch),
        compiler_params=pltpu.CompilerParams(vmem_limit_bytes=limit * 2**20),
        cost_estimate=pl.CostEstimate(flops=cost[0], bytes_accessed=cost[1], transcendentals=0),
    )(*args)


def gram_kernel(grads_hbm, out_ref, grads_ref, whole_ref, in_sems, out_sems):
    shards, size, _ = grads_ref.shape
    xs, zs, double, _ = out_ref.shape
    rows = double // 2
    loads = [pltpu.make_async_copy(grads_hbm.at[s], grads_ref.at[s], in_sems.at[s]) for s in range(shards)]
    for load in loads:
        load.start()
    for load in loads:
        load.wait()
    stores = []
    half = size // 2
    for h in range(2):
        gram = None
        total = None
        for s in range(shards):
            mine = grads_ref[s, h * half : (h + 1) * half]
            term = lax.dot_general(mine, grads_ref[s], (((1,), (1,)), ((), ())), preferred_element_type=f32)
            gram = term if gram is None else gram + term
            wide = mine.astype(f32)
            total = wide if total is None else total + wide
        gram = gram.reshape(zs // 2, xs, rows, size)
        total = total.reshape(zs // 2, xs, rows, size)
        part = slice(h * zs // 2, (h + 1) * zs // 2)
        for x in range(xs):
            whole_ref[x, part, :rows, :] = gram[:, x]
            whole_ref[x, part, rows:, :] = total[:, x]
            stores.append(pltpu.make_async_copy(whole_ref.at[x, part], out_ref.at[x, part], out_sems.at[h, x]))
            stores[-1].start()
    for store in stores:
        store.wait()


def sum_kernel(parts_ref, after_ref, out_ref):
    del after_ref
    out_ref[...] = jnp.sum(parts_ref[...], axis=0)


def choose(k, options):
    value = options[0]
    for i in range(1, len(options)):
        value = jnp.where(k == i, options[i], value)
    return value


def table_kernel(me_ref, owner_ref, out_ref, count_ref, slot_ref, block_ref):
    blocks = owner_ref.shape[0]
    me = me_ref[0]
    y, q = me >> 2, me & 3
    for b in range(blocks):
        count_ref[b] = 0
    for i in range(9):
        block_ref[i] = -1
    for b in range(blocks):
        o = owner_ref[b]
        s = jnp.minimum(count_ref[o], 1)
        count_ref[o] = s + 1
        slot_ref[b] = s
        near = o ^ me
        block_ref[jnp.where(near < 4, near * 2 + s, 8)] = b

    def put(i, block, line, last=False):
        o = owner_ref[block]
        d = ((o ^ me) >> 2) & 3
        which = jnp.where(d == 0, (((o ^ q) >> 1) & 1) + 2 * ((o ^ q) & 1), 3 + d)
        if last:
            which = jnp.where((o >> 4) == (me >> 4), which, 7)
        out_ref[i * ENTRY] = which
        out_ref[i * ENTRY + 1] = slot_ref[block]
        out_ref[i * ENTRY + 2] = line

    for n in range(1, 4):
        for t in range(2):
            put((n - 1) * 2 + t, (((y & 3) ^ n) + 4 * t) * GROUP + q, t)
    put(6, me ^ 16, (me >> 4) ^ 1)
    put(7, me, me >> 4, True)
    for i in range(8):
        block = block_ref[i]
        out_ref[RETURN + 3 * i] = ((block ^ me) >> 2) & 1
        out_ref[RETURN + 3 * i + 1] = (((block ^ me) >> 4) & 1) + 2 * (((block ^ me) >> 3) & 1)
        out_ref[RETURN + 3 * i + 2] = jnp.where(block < 0, -1, (block ^ me) & 3)


def columns(place, rows, size):
    first = place * rows // LANES
    return [pl.multiple_of((first + n) % (size // LANES) * LANES, LANES) for n in range(size // LANES - 1)]


def keep_kernel(place_ref, held_ref, held_z_ref, kept_ref):
    capacity, rows, size = held_ref.shape
    for n, column in enumerate(columns(place_ref[0], rows, size)):
        for i, held in enumerate((held_ref, held_z_ref)):
            for j in range(capacity):
                kept_ref[i, j, :, n * LANES : (n + 1) * LANES] = held[j, :, pl.ds(column, LANES)]


def pick(table_ref, entry, kept_ref, core_ref, near=(), far=()):
    which, slot, line = (table_ref[entry * ENTRY + i] for i in range(ENTRY))
    options = [k[i, slot] for k in (kept_ref, core_ref) for i in range(2)]
    return choose(which, options + [g[line] for g in near] + [g[...] for g in far])


def near_kernel(table_ref, kept_ref, core_ref, *outs):
    for n, out in enumerate(outs):
        for t in range(2):
            out[t] = pick(table_ref, n * 2 + t, kept_ref, core_ref)


def far_kernel(table_ref, kept_ref, core_ref, near1, near2, near3, out_ref):
    out_ref[...] = pick(table_ref, 6, kept_ref, core_ref, (near1, near2, near3))


def packed_rows(rows, size):
    return 2 * rows + rows // 2 + size // LANES * rows


def stat_kernel(table_ref, place_ref, sums_ref, kept_ref, core_ref, *refs):
    wide_ref, gram_ref, stat_ref, both_ref = refs[4:]
    _, rows, size = gram_ref.shape
    sums = jnp.sum(sums_ref[...], axis=0)
    gram_ref[0] = sums[:rows]
    for n, column in enumerate(columns(place_ref[0], rows, size)):
        stat_ref[:, n * LANES : (n + 1) * LANES] = gram_ref[0, :, pl.ds(column, LANES)]
    stat = stat_ref[...] + pick(table_ref, 7, kept_ref, core_ref, refs[:3], refs[3:4])
    both_ref[:rows] = stat[:, :LANES]
    both_ref[rows : 2 * rows] = stat[:, LANES : 2 * LANES]
    x, z = place_ref[0] % ACROSS, place_ref[0] // ACROSS
    third = [stat[:, 2 * LANES + s * rows : 2 * LANES + (s + 1) * rows] for s in range(LANES // rows)]
    odd = (x + z // 2) % 2
    half = jnp.where(odd == 0, jnp.concatenate(third[::2], axis=1), jnp.concatenate(third[1::2], axis=1))
    half = jnp.concatenate([half[: rows // 2], half[rows // 2 :]], axis=1)
    start = 2 * rows + rows // 2
    both_ref[2 * rows : start] = half
    for m in range(size // LANES):
        both_ref[start + m * rows : start + (m + 1) * rows] = sums[rows:, m * LANES : (m + 1) * LANES]
    wide_ref[...] = jnp.broadcast_to(both_ref[...][None], wide_ref.shape)


def stack_kernel(first_ref, second_ref, out_ref):
    half = out_ref.shape[0] // 2
    out_ref[:half] = first_ref[...]
    out_ref[half:] = second_ref[...]


def return_kernel(table_ref, line_ref, far_ref, *outs):
    for i in range(8):
        n, line = table_ref[RETURN + 3 * i], table_ref[RETURN + 3 * i + 1]
        outs[i // 2][i % 2] = choose(n, [line_ref[line], far_ref[line]])


def state_kernel(table_ref, state_ref, got0, got1, got2, got3, after_ref, out_ref):
    del after_ref
    for j in range(2):
        way = table_ref[RETURN + 3 * j + 2]
        gram = choose(way, [got0[j], got1[j], got2[j], got3[j]])
        out_ref[j] = state_ref[j] + jnp.where(way >= 0, gram, 0.0)


def split(a):
    high = a.astype(bf16)
    return high, (a - high.astype(f32)).astype(bf16)


def product(a, b):
    (a_high, a_low), (b_high, b_low) = a, b
    half = a_high.shape[0] // 2
    left = jnp.concatenate([a_high, a_high, a_low], axis=1)
    right = jnp.concatenate([b_high, b_low, b_high], axis=0)
    top = jnp.dot(left[:half], right, preferred_element_type=f32)
    corner = jnp.dot(left[half:], right[:, half:], preferred_element_type=f32)
    return jnp.concatenate([top, jnp.concatenate([top[:, half:].T, corner], axis=1)], axis=0)


def copies_kernel(part_ref, after_ref, out_ref, sems):
    del after_ref
    copies = [pltpu.make_async_copy(part_ref, out_ref.at[x], sems.at[x]) for x in range(out_ref.shape[0])]
    for copy in copies:
        copy.start()
    for copy in copies:
        copy.wait()


def thin_product(a, b):
    a_high, a_low = split(a)
    rows = a.shape[0]
    both = jnp.dot(jnp.concatenate([a_high, a_low], axis=0), b[0], preferred_element_type=f32)
    return both[:rows] + (both[rows:] + jnp.dot(a_high, b[1], preferred_element_type=f32))


def newton_kernel(count, place_ref, all_ref, after_ref, out_ref, end_ref, stat_ref):
    del after_ref
    end_ref[...] = jnp.zeros_like(end_ref)
    xs, zs, _, _ = all_ref.shape
    size = stat_ref.shape[1]
    rows = size // (xs * zs)
    start = 2 * rows + rows // 2
    place = place_ref[0]
    block = lambda i: slice(i % zs * LANES, (i % zs + 1) * LANES)
    third = []
    for z in range(zs):
        for n in range(2):
            part = jnp.concatenate([all_ref[x, z, n * rows : (n + 1) * rows] for x in range(xs)], axis=0)
            stat_ref[block(z), block(z + n)] = part
            if n == 1:
                stat_ref[block(z + n), block(z)] = part.T
        strips = []
        for x in range(xs):
            half = all_ref[x, z, 2 * rows : start]
            half = jnp.concatenate([half[:, : LANES // 2], half[:, LANES // 2 :]], axis=0)
            blank = jnp.zeros((rows, rows), f32)
            pieces = [half[:, :rows], blank, half[:, rows:], blank]
            strips.append(jnp.concatenate(pieces if (x + z // 2) % 2 == 0 else pieces[1:2] + pieces[:1] + pieces[3:] + pieces[2:3], axis=1))
        third.append(jnp.concatenate(strips, axis=0))
    for z in range(zs // 2):
        part = third[z] + third[z + 2].T
        stat_ref[block(z), block(z + 2)] = part
        stat_ref[block(z + 2), block(z)] = part.T
    stat = stat_ref[...]
    diagonal = lax.broadcasted_iota(jnp.int32, (size, size), 0) == lax.broadcasted_iota(jnp.int32, (size, size), 1)
    plus = lambda a, m: jnp.where(diagonal, m + a, m)
    thin_rows = lax.broadcasted_iota(jnp.int32, (rows, size), 0) + place * rows
    thin_cols = lax.broadcasted_iota(jnp.int32, (rows, size), 1)
    thin_eye = (thin_rows == thin_cols).astype(f32)
    norm = jnp.sqrt(jnp.sum(stat * stat))
    damped = plus(DAMP * norm, stat)
    scale = jnp.sqrt(jnp.sum(damped * damped))
    iterate = damped / scale
    mine = stat_ref[pl.ds(pl.multiple_of(place * rows, rows), rows), :]
    mine = (mine + (DAMP * norm) * thin_eye) / scale
    thin = 1.25 * thin_eye - 0.25 * mine
    parts_of = split(iterate)
    for _ in range(ITERS - 2):
        square = product(parts_of, parts_of)
        factor2 = split(plus(1.5625, 0.0625 * square - 0.625 * iterate))
        iterate = product(parts_of, split(product(factor2, factor2)))
        parts_of = split(iterate)
        thin = 1.25 * thin - 0.25 * thin_product(thin, parts_of)
    last = thin_product(thin, parts_of)
    for _ in range(4):
        last = 1.25 * last - 0.25 * thin_product(last, parts_of)
    thin = (1.25 * thin - 0.25 * last) * jnp.exp(-0.25 * jnp.log(scale))
    mean = [
        jnp.concatenate(
            [all_ref[x, z, start + m * rows : start + (m + 1) * rows] for z in range(zs) for x in range(xs)], axis=0
        )
        for m in range(size // LANES)
    ]
    mean = (jnp.concatenate(mean, axis=1) / count).astype(bf16)
    out_ref[0] = jnp.dot(thin.astype(bf16), mean, preferred_element_type=f32).astype(bf16)


def body(grads, owner, state):
    local = grads[:, 0]
    shards, size, _ = local.shape
    held = state[0]
    capacity, rows, _ = held.shape
    reps = lax.axis_size("rep")
    blocks = owner.shape[0]
    groups = blocks // GROUP
    shape = lambda *s: jax.ShapeDtypeStruct(s, f32)

    def across(x, k):
        return lax.ppermute(x, "pre", [(i, i ^ k) for i in range(blocks)])

    zs = reps // ACROSS
    x_groups = [[z * ACROSS + x for x in range(ACROSS)] for z in range(zs)]
    z_groups = [[z * ACROSS + x for z in range(zs)] for x in range(ACROSS)]

    def exchange(x, which):
        return lax.all_to_all(x, "rep", 0, 0, tiled=True, axis_index_groups=which)

    me = lax.axis_index("pre").reshape(1).astype(jnp.int32)
    place = lax.axis_index("rep").reshape(1).astype(jnp.int32)
    table = pl.pallas_call(
        table_kernel,
        out_shape=jax.ShapeDtypeStruct((RETURN + 24,), jnp.int32),
        in_specs=[SMEM, SMEM],
        out_specs=SMEM,
        scratch_shapes=[
            pltpu.SMEM((blocks,), jnp.int32),
            pltpu.SMEM((blocks,), jnp.int32),
            pltpu.SMEM((16,), jnp.int32),
        ],
    )(me, owner)

    held_z = across(held, 2)
    sums = call(
        gram_kernel,
        shape(ACROSS, zs, 2 * rows, size),
        [ANY],
        (2 * shards * size**3, 4 * size * size * (shards + 2)),
        local,
        limit=60,
        out_specs=ANY,
        scratch=[
            pltpu.VMEM(local.shape, local.dtype),
            pltpu.VMEM((ACROSS, zs, 2 * rows, size), f32),
            pltpu.SemaphoreType.DMA((shards,)),
            pltpu.SemaphoreType.DMA((2, ACROSS)),
        ],
    )
    sums = exchange(sums, x_groups)
    kept = call(
        keep_kernel,
        shape(2, capacity, rows, size - LANES),
        [SMEM, VMEM, VMEM],
        (2 * 100 * size**3, 4 * size * rows * 8),
        place,
        held,
        held_z,
    )
    core = across(kept, 1)
    near = call(
        near_kernel,
        [shape(2, rows, size - LANES)] * 3,
        [SMEM, VMEM, VMEM],
        (0, 4 * size * rows * 12),
        table,
        kept,
        core,
    )
    near = [across(sent, GROUP * (n + 1)) for n, sent in enumerate(near)]
    far = call(
        far_kernel,
        shape(rows, size - LANES),
        [SMEM] + [VMEM] * 5,
        (0, 4 * size * rows * 12),
        table,
        kept,
        core,
        *near,
    )
    sums = call(
        sum_kernel,
        shape(zs, 2 * rows, size),
        [VMEM, ANY],
        (0, 4 * size * rows * 40),
        sums,
        far,
    )
    sums = exchange(sums, z_groups)
    far = across(far, 4 * GROUP)
    both, gram = call(
        stat_kernel,
        [shape(zs, packed_rows(rows, size), LANES), shape(1, rows, size)],
        [SMEM, SMEM] + [VMEM] * 7,
        (0, 4 * size * rows * 45),
        table,
        place,
        sums,
        kept,
        core,
        *near,
        far,
        scratch=[
            pltpu.VMEM((rows, size - LANES), f32),
            pltpu.VMEM((packed_rows(rows, size), LANES), f32),
        ],
    )
    both = exchange(both, z_groups)
    line = gram
    lines = []
    for bit in (4, 2):
        line = call(
            stack_kernel,
            shape(2 * line.shape[0], rows, size),
            [VMEM] * 2,
            (2 * (60 if bit == 2 else 0) * size**3, 4 * size * rows * 8),
            line,
            across(line, GROUP * bit),
        )
        lines.append(line)
    both = call(
        copies_kernel,
        shape(ACROSS, zs, packed_rows(rows, size), LANES),
        [VMEM, ANY],
        (0, 4 * size * rows * 40),
        both,
        lines[0],
        out_specs=HBM,
        scratch=[pltpu.SemaphoreType.DMA((ACROSS,))],
    )
    both = exchange(both, x_groups)
    own, *sent = call(
        return_kernel,
        [shape(capacity, rows, size)] * 4,
        [SMEM] + [VMEM] * 2,
        (0, 4 * size * rows * 24),
        table,
        line,
        across(line, GROUP),
    )
    count = shards * reps
    update, end = call(
        functools.partial(newton_kernel, count),
        [jax.ShapeDtypeStruct((1, rows, size), bf16), shape(8, LANES)],
        [SMEM, VMEM, ANY],
        (2 * 20 * size**3, 8 * size * size),
        place,
        both,
        own,
        scratch=[pltpu.VMEM((size, size), f32)],
    )
    new_state = call(
        state_kernel,
        shape(capacity, rows, size),
        [SMEM] + [VMEM] * 5 + [ANY],
        (0, 4 * size * rows * 8),
        table,
        held,
        own,
        *[across(rows_sent, k + 1) for k, rows_sent in enumerate(sent)],
        end,
    )
    return (new_state[None], update)


def solution(mesh):
    placed = (P("rep", "pre", None, None), P(), P("pre", None, "rep", None))
    return jax.shard_map(
        body,
        mesh=mesh,
        in_specs=placed,
        out_specs=(P("pre", None, "rep", None), P("pre", "rep", None)),
        check_vma=False,
    )
```

```python
import functools

import jax
import jax.numpy as jnp
from jax import lax
from jax.experimental import pallas as pl
from jax.experimental.pallas import tpu as pltpu
from jax.sharding import PartitionSpec as P

ITERS = 4
DAMP = 0.05
GROUP = 4
LANES = 128
ENTRY = 3
RETURN = 8 * ENTRY
ACROSS = 4
f32 = jnp.float32
bf16 = jnp.bfloat16

VMEM = pl.BlockSpec(memory_space=pltpu.VMEM)
ANY = pl.BlockSpec(memory_space=pl.ANY)
HBM = pl.BlockSpec(memory_space=pltpu.HBM)
SMEM = pl.BlockSpec(memory_space=pltpu.SMEM)


def call(kernel, out_shape, in_specs, cost, *args, scratch=(), out_specs=VMEM, limit=40):
    multiple = isinstance(out_shape, (list, tuple))
    return pl.pallas_call(
        kernel,
        out_shape=out_shape,
        in_specs=in_specs,
        out_specs=[out_specs] * len(out_shape) if multiple else out_specs,
        scratch_shapes=list(scratch),
        compiler_params=pltpu.CompilerParams(vmem_limit_bytes=limit * 2**20),
        cost_estimate=pl.CostEstimate(flops=cost[0], bytes_accessed=cost[1], transcendentals=0),
    )(*args)


def gram_kernel(grads_hbm, out_ref, grads_ref, whole_ref, in_sems, out_sems):
    shards, size, _ = grads_ref.shape
    xs, zs, double, _ = out_ref.shape
    rows = double // 2
    loads = [pltpu.make_async_copy(grads_hbm.at[s], grads_ref.at[s], in_sems.at[s]) for s in range(shards)]
    for load in loads:
        load.start()
    for load in loads:
        load.wait()
    stores = []
    half = size // 2
    for h in range(2):
        gram = None
        total = None
        for s in range(shards):
            mine = grads_ref[s, h * half : (h + 1) * half]
            term = lax.dot_general(mine, grads_ref[s], (((1,), (1,)), ((), ())), preferred_element_type=f32)
            gram = term if gram is None else gram + term
            wide = mine.astype(f32)
            total = wide if total is None else total + wide
        gram = gram.reshape(zs // 2, xs, rows, size)
        total = total.reshape(zs // 2, xs, rows, size)
        part = slice(h * zs // 2, (h + 1) * zs // 2)
        for x in range(xs):
            whole_ref[x, part, :rows, :] = gram[:, x]
            whole_ref[x, part, rows:, :] = total[:, x]
            stores.append(pltpu.make_async_copy(whole_ref.at[x, part], out_ref.at[x, part], out_sems.at[h, x]))
            stores[-1].start()
    for store in stores:
        store.wait()


def sum_kernel(parts_ref, after_ref, out_ref):
    del after_ref
    out_ref[...] = jnp.sum(parts_ref[...], axis=0)


def choose(k, options):
    value = options[0]
    for i in range(1, len(options)):
        value = jnp.where(k == i, options[i], value)
    return value


def table_kernel(me_ref, owner_ref, out_ref, count_ref, slot_ref, block_ref):
    blocks = owner_ref.shape[0]
    me = me_ref[0]
    y, q = me >> 2, me & 3
    for b in range(blocks):
        count_ref[b] = 0
    for i in range(9):
        block_ref[i] = -1
    for b in range(blocks):
        o = owner_ref[b]
        s = jnp.minimum(count_ref[o], 1)
        count_ref[o] = s + 1
        slot_ref[b] = s
        near = o ^ me
        block_ref[jnp.where(near < 4, near * 2 + s, 8)] = b

    def put(i, block, line, last=False):
        o = owner_ref[block]
        d = ((o ^ me) >> 2) & 3
        which = jnp.where(d == 0, (((o ^ q) >> 1) & 1) + 2 * ((o ^ q) & 1), 3 + d)
        if last:
            which = jnp.where((o >> 4) == (me >> 4), which, 7)
        out_ref[i * ENTRY] = which
        out_ref[i * ENTRY + 1] = slot_ref[block]
        out_ref[i * ENTRY + 2] = line

    for n in range(1, 4):
        for t in range(2):
            put((n - 1) * 2 + t, (((y & 3) ^ n) + 4 * t) * GROUP + q, t)
    put(6, me ^ 16, (me >> 4) ^ 1)
    put(7, me, me >> 4, True)
    for i in range(8):
        block = block_ref[i]
        out_ref[RETURN + 3 * i] = ((block ^ me) >> 2) & 1
        out_ref[RETURN + 3 * i + 1] = (((block ^ me) >> 4) & 1) + 2 * (((block ^ me) >> 3) & 1)
        out_ref[RETURN + 3 * i + 2] = jnp.where(block < 0, -1, (block ^ me) & 3)


def columns(place, rows, size):
    first = place * rows // LANES
    return [pl.multiple_of((first + n) % (size // LANES) * LANES, LANES) for n in range(size // LANES - 1)]


def keep_kernel(place_ref, held_ref, held_z_ref, kept_ref):
    capacity, rows, size = held_ref.shape
    for n, column in enumerate(columns(place_ref[0], rows, size)):
        for i, held in enumerate((held_ref, held_z_ref)):
            for j in range(capacity):
                kept_ref[i, j, :, n * LANES : (n + 1) * LANES] = held[j, :, pl.ds(column, LANES)]


def pick(table_ref, entry, kept_ref, core_ref, near=(), far=()):
    which, slot, line = (table_ref[entry * ENTRY + i] for i in range(ENTRY))
    options = [k[i, slot] for k in (kept_ref, core_ref) for i in range(2)]
    return choose(which, options + [g[line] for g in near] + [g[...] for g in far])


def near_kernel(table_ref, kept_ref, core_ref, *outs):
    for n, out in enumerate(outs):
        for t in range(2):
            out[t] = pick(table_ref, n * 2 + t, kept_ref, core_ref)


def far_kernel(table_ref, kept_ref, core_ref, near1, near2, near3, out_ref):
    out_ref[...] = pick(table_ref, 6, kept_ref, core_ref, (near1, near2, near3))


def packed_rows(rows, size):
    return 2 * rows + rows // 2 + size // LANES * rows


def stat_kernel(table_ref, place_ref, sums_ref, kept_ref, core_ref, *refs):
    wide_ref, gram_ref, stat_ref, both_ref = refs[4:]
    _, rows, size = gram_ref.shape
    sums = jnp.sum(sums_ref[...], axis=0)
    gram_ref[0] = sums[:rows]
    for n, column in enumerate(columns(place_ref[0], rows, size)):
        stat_ref[:, n * LANES : (n + 1) * LANES] = gram_ref[0, :, pl.ds(column, LANES)]
    stat = stat_ref[...] + pick(table_ref, 7, kept_ref, core_ref, refs[:3], refs[3:4])
    both_ref[:rows] = stat[:, :LANES]
    both_ref[rows : 2 * rows] = stat[:, LANES : 2 * LANES]
    x, z = place_ref[0] % ACROSS, place_ref[0] // ACROSS
    third = [stat[:, 2 * LANES + s * rows : 2 * LANES + (s + 1) * rows] for s in range(LANES // rows)]
    odd = (x + z // 2) % 2
    half = jnp.where(odd == 0, jnp.concatenate(third[::2], axis=1), jnp.concatenate(third[1::2], axis=1))
    half = jnp.concatenate([half[: rows // 2], half[rows // 2 :]], axis=1)
    start = 2 * rows + rows // 2
    both_ref[2 * rows : start] = half
    for m in range(size // LANES):
        both_ref[start + m * rows : start + (m + 1) * rows] = sums[rows:, m * LANES : (m + 1) * LANES]
    wide_ref[...] = jnp.broadcast_to(both_ref[...][None], wide_ref.shape)


def stack_kernel(first_ref, second_ref, out_ref):
    half = out_ref.shape[0] // 2
    out_ref[:half] = first_ref[...]
    out_ref[half:] = second_ref[...]


def return_kernel(table_ref, line_ref, far_ref, *outs):
    for i in range(8):
        n, line = table_ref[RETURN + 3 * i], table_ref[RETURN + 3 * i + 1]
        outs[i // 2][i % 2] = choose(n, [line_ref[line], far_ref[line]])


def state_kernel(table_ref, state_ref, got0, got1, got2, got3, after_ref, out_ref):
    del after_ref
    for j in range(2):
        way = table_ref[RETURN + 3 * j + 2]
        gram = choose(way, [got0[j], got1[j], got2[j], got3[j]])
        out_ref[j] = state_ref[j] + jnp.where(way >= 0, gram, 0.0)


def split(a):
    high = a.astype(bf16)
    return high, (a - high.astype(f32)).astype(bf16)


def product(a, b):
    (a_high, a_low), (b_high, b_low) = a, b
    half = a_high.shape[0] // 2
    left = jnp.concatenate([a_high, a_high, a_low], axis=1)
    right = jnp.concatenate([b_high, b_low, b_high], axis=0)
    top = jnp.dot(left[:half], right, preferred_element_type=f32)
    corner = jnp.dot(left[half:], right[:, half:], preferred_element_type=f32)
    return jnp.concatenate([top, jnp.concatenate([top[:, half:].T, corner], axis=1)], axis=0)


def copies_kernel(part_ref, after_ref, out_ref, sems):
    del after_ref
    copies = [pltpu.make_async_copy(part_ref, out_ref.at[x], sems.at[x]) for x in range(out_ref.shape[0])]
    for copy in copies:
        copy.start()
    for copy in copies:
        copy.wait()


def thin_product(a, b):
    a_high, a_low = split(a)
    rows = a.shape[0]
    both = jnp.dot(jnp.concatenate([a_high, a_low], axis=0), b[0], preferred_element_type=f32)
    return both[:rows] + (both[rows:] + jnp.dot(a_high, b[1], preferred_element_type=f32))


def newton_kernel(count, place_ref, all_ref, after_ref, out_ref, end_ref, stat_ref):
    del after_ref
    end_ref[...] = jnp.zeros_like(end_ref)
    xs, zs, _, _ = all_ref.shape
    size = stat_ref.shape[1]
    rows = size // (xs * zs)
    start = 2 * rows + rows // 2
    place = place_ref[0]
    block = lambda i: slice(i % zs * LANES, (i % zs + 1) * LANES)
    third = []
    for z in range(zs):
        for n in range(2):
            part = jnp.concatenate([all_ref[x, z, n * rows : (n + 1) * rows] for x in range(xs)], axis=0)
            stat_ref[block(z), block(z + n)] = part
            if n == 1:
                stat_ref[block(z + n), block(z)] = part.T
        strips = []
        for x in range(xs):
            half = all_ref[x, z, 2 * rows : start]
            half = jnp.concatenate([half[:, : LANES // 2], half[:, LANES // 2 :]], axis=0)
            blank = jnp.zeros((rows, rows), f32)
            pieces = [half[:, :rows], blank, half[:, rows:], blank]
            strips.append(jnp.concatenate(pieces if (x + z // 2) % 2 == 0 else pieces[1:2] + pieces[:1] + pieces[3:] + pieces[2:3], axis=1))
        third.append(jnp.concatenate(strips, axis=0))
    for z in range(zs // 2):
        part = third[z] + third[z + 2].T
        stat_ref[block(z), block(z + 2)] = part
        stat_ref[block(z + 2), block(z)] = part.T
    stat = stat_ref[...]
    diagonal = lax.broadcasted_iota(jnp.int32, (size, size), 0) == lax.broadcasted_iota(jnp.int32, (size, size), 1)
    plus = lambda a, m: jnp.where(diagonal, m + a, m)
    thin_rows = lax.broadcasted_iota(jnp.int32, (rows, size), 0) + place * rows
    thin_cols = lax.broadcasted_iota(jnp.int32, (rows, size), 1)
    thin_eye = (thin_rows == thin_cols).astype(f32)
    squares = jnp.sum(stat * stat)
    trace = jnp.sum(jnp.where(diagonal, stat, 0.0))
    norm = jnp.sqrt(squares)
    damp = DAMP * norm
    scale = jnp.sqrt(squares + 2.0 * damp * trace + size * damp * damp)
    iterate = plus(damp, stat) * (1.0 / scale)
    mine = stat_ref[pl.ds(pl.multiple_of(place * rows, rows), rows), :]
    mine = (mine + damp * thin_eye) * (1.0 / scale)
    thin = 1.25 * thin_eye - 0.25 * mine
    parts_of = split(iterate)
    for _ in range(ITERS - 2):
        square = product(parts_of, parts_of)
        factor2 = split(plus(1.5625, 0.0625 * square - 0.625 * iterate))
        iterate = product(parts_of, split(product(factor2, factor2)))
        parts_of = split(iterate)
        thin = 1.25 * thin - 0.25 * thin_product(thin, parts_of)
    last = thin_product(thin, parts_of)
    for _ in range(4):
        last = 1.25 * last - 0.25 * thin_product(last, parts_of)
    thin = (1.25 * thin - 0.25 * last) * jnp.exp(-0.25 * jnp.log(scale))
    mean = [
        jnp.concatenate(
            [all_ref[x, z, start + m * rows : start + (m + 1) * rows] for z in range(zs) for x in range(xs)], axis=0
        )
        for m in range(size // LANES)
    ]
    mean = (jnp.concatenate(mean, axis=1) * (1.0 / count)).astype(bf16)
    out_ref[0] = jnp.dot(thin.astype(bf16), mean, preferred_element_type=f32).astype(bf16)


def body(grads, owner, state):
    local = grads[:, 0]
    shards, size, _ = local.shape
    held = state[0]
    capacity, rows, _ = held.shape
    reps = lax.axis_size("rep")
    blocks = owner.shape[0]
    groups = blocks // GROUP
    shape = lambda *s: jax.ShapeDtypeStruct(s, f32)

    def across(x, k):
        return lax.ppermute(x, "pre", [(i, i ^ k) for i in range(blocks)])

    zs = reps // ACROSS
    x_groups = [[z * ACROSS + x for x in range(ACROSS)] for z in range(zs)]
    z_groups = [[z * ACROSS + x for z in range(zs)] for x in range(ACROSS)]

    def exchange(x, which):
        return lax.all_to_all(x, "rep", 0, 0, tiled=True, axis_index_groups=which)

    me = lax.axis_index("pre").reshape(1).astype(jnp.int32)
    place = lax.axis_index("rep").reshape(1).astype(jnp.int32)
    table = pl.pallas_call(
        table_kernel,
        out_shape=jax.ShapeDtypeStruct((RETURN + 24,), jnp.int32),
        in_specs=[SMEM, SMEM],
        out_specs=SMEM,
        scratch_shapes=[
            pltpu.SMEM((blocks,), jnp.int32),
            pltpu.SMEM((blocks,), jnp.int32),
            pltpu.SMEM((16,), jnp.int32),
        ],
    )(me, owner)

    held_z = across(held, 2)
    sums = call(
        gram_kernel,
        shape(ACROSS, zs, 2 * rows, size),
        [ANY],
        (2 * shards * size**3, 4 * size * size * (shards + 2)),
        local,
        limit=60,
        out_specs=ANY,
        scratch=[
            pltpu.VMEM(local.shape, local.dtype),
            pltpu.VMEM((ACROSS, zs, 2 * rows, size), f32),
            pltpu.SemaphoreType.DMA((shards,)),
            pltpu.SemaphoreType.DMA((2, ACROSS)),
        ],
    )
    sums = exchange(sums, x_groups)
    kept = call(
        keep_kernel,
        shape(2, capacity, rows, size - LANES),
        [SMEM, VMEM, VMEM],
        (2 * 100 * size**3, 4 * size * rows * 8),
        place,
        held,
        held_z,
    )
    core = across(kept, 1)
    near = call(
        near_kernel,
        [shape(2, rows, size - LANES)] * 3,
        [SMEM, VMEM, VMEM],
        (0, 4 * size * rows * 12),
        table,
        kept,
        core,
    )
    near = [across(sent, GROUP * (n + 1)) for n, sent in enumerate(near)]
    far = call(
        far_kernel,
        shape(rows, size - LANES),
        [SMEM] + [VMEM] * 5,
        (0, 4 * size * rows * 12),
        table,
        kept,
        core,
        *near,
    )
    sums = call(
        sum_kernel,
        shape(zs, 2 * rows, size),
        [VMEM, ANY],
        (0, 4 * size * rows * 40),
        sums,
        far,
    )
    sums = exchange(sums, z_groups)
    far = across(far, 4 * GROUP)
    both, gram = call(
        stat_kernel,
        [shape(zs, packed_rows(rows, size), LANES), shape(1, rows, size)],
        [SMEM, SMEM] + [VMEM] * 7,
        (0, 4 * size * rows * 45),
        table,
        place,
        sums,
        kept,
        core,
        *near,
        far,
        scratch=[
            pltpu.VMEM((rows, size - LANES), f32),
            pltpu.VMEM((packed_rows(rows, size), LANES), f32),
        ],
    )
    both = exchange(both, z_groups)
    line = gram
    lines = []
    for bit in (4, 2):
        line = call(
            stack_kernel,
            shape(2 * line.shape[0], rows, size),
            [VMEM] * 2,
            (2 * (60 if bit == 2 else 0) * size**3, 4 * size * rows * 8),
            line,
            across(line, GROUP * bit),
        )
        lines.append(line)
    both = call(
        copies_kernel,
        shape(ACROSS, zs, packed_rows(rows, size), LANES),
        [VMEM, ANY],
        (0, 4 * size * rows * 40),
        both,
        lines[0],
        out_specs=HBM,
        scratch=[pltpu.SemaphoreType.DMA((ACROSS,))],
    )
    both = exchange(both, x_groups)
    own, *sent = call(
        return_kernel,
        [shape(capacity, rows, size)] * 4,
        [SMEM] + [VMEM] * 2,
        (0, 4 * size * rows * 24),
        table,
        line,
        across(line, GROUP),
    )
    count = shards * reps
    update, end = call(
        functools.partial(newton_kernel, count),
        [jax.ShapeDtypeStruct((1, rows, size), bf16), shape(8, LANES)],
        [SMEM, VMEM, ANY],
        (2 * 20 * size**3, 8 * size * size),
        place,
        both,
        own,
        scratch=[pltpu.VMEM((size, size), f32)],
    )
    new_state = call(
        state_kernel,
        shape(capacity, rows, size),
        [SMEM] + [VMEM] * 5 + [ANY],
        (0, 4 * size * rows * 8),
        table,
        held,
        own,
        *[across(rows_sent, k + 1) for k, rows_sent in enumerate(sent)],
        end,
    )
    return (new_state[None], update)


def solution(mesh):
    placed = (P("rep", "pre", None, None), P(), P("pre", None, "rep", None))
    return jax.shard_map(
        body,
        mesh=mesh,
        in_specs=placed,
        out_specs=(P("pre", None, "rep", None), P("pre", "rep", None)),
        check_vma=False,
    )
```

```python
import functools

import jax
import jax.numpy as jnp
from jax import lax
from jax.experimental import pallas as pl
from jax.experimental.pallas import tpu as pltpu
from jax.sharding import PartitionSpec as P

ITERS = 4
DAMP = 0.05
GROUP = 4
LANES = 128
ENTRY = 3
RETURN = 8 * ENTRY
ACROSS = 4
f32 = jnp.float32
bf16 = jnp.bfloat16

VMEM = pl.BlockSpec(memory_space=pltpu.VMEM)
ANY = pl.BlockSpec(memory_space=pl.ANY)
HBM = pl.BlockSpec(memory_space=pltpu.HBM)
SMEM = pl.BlockSpec(memory_space=pltpu.SMEM)


def call(kernel, out_shape, in_specs, cost, *args, scratch=(), out_specs=VMEM, limit=40):
    multiple = isinstance(out_shape, (list, tuple))
    return pl.pallas_call(
        kernel,
        out_shape=out_shape,
        in_specs=in_specs,
        out_specs=[out_specs] * len(out_shape) if multiple else out_specs,
        scratch_shapes=list(scratch),
        compiler_params=pltpu.CompilerParams(vmem_limit_bytes=limit * 2**20),
        cost_estimate=pl.CostEstimate(flops=cost[0], bytes_accessed=cost[1], transcendentals=0),
    )(*args)


def gram_kernel(grads_ref, out_ref, whole_ref, out_sems):
    shards, size, _ = grads_ref.shape
    xs, zs, double, _ = out_ref.shape
    rows = double // 2
    stores = []
    half = size // 2
    for h in range(2):
        gram = None
        total = None
        for s in range(shards):
            mine = grads_ref[s, h * half : (h + 1) * half]
            term = lax.dot_general(mine, grads_ref[s], (((1,), (1,)), ((), ())), preferred_element_type=f32)
            gram = term if gram is None else gram + term
            wide = mine.astype(f32)
            total = wide if total is None else total + wide
        gram = gram.reshape(zs // 2, xs, rows, size)
        total = total.reshape(zs // 2, xs, rows, size)
        part = slice(h * zs // 2, (h + 1) * zs // 2)
        for x in range(xs):
            whole_ref[x, part, :rows, :] = gram[:, x]
            whole_ref[x, part, rows:, :] = total[:, x]
            stores.append(pltpu.make_async_copy(whole_ref.at[x, part], out_ref.at[x, part], out_sems.at[h, x]))
            stores[-1].start()
    for store in stores:
        store.wait()


def sum_kernel(parts_ref, after_ref, out_ref):
    del after_ref
    out_ref[...] = jnp.sum(parts_ref[...], axis=0)


def choose(k, options):
    value = options[0]
    for i in range(1, len(options)):
        value = jnp.where(k == i, options[i], value)
    return value


def table_kernel(me_ref, owner_ref, out_ref, count_ref, slot_ref, block_ref):
    blocks = owner_ref.shape[0]
    me = me_ref[0]
    y, q = me >> 2, me & 3
    for b in range(blocks):
        count_ref[b] = 0
    for i in range(9):
        block_ref[i] = -1
    for b in range(blocks):
        o = owner_ref[b]
        s = jnp.minimum(count_ref[o], 1)
        count_ref[o] = s + 1
        slot_ref[b] = s
        near = o ^ me
        block_ref[jnp.where(near < 4, near * 2 + s, 8)] = b

    def put(i, block, line, last=False):
        o = owner_ref[block]
        d = ((o ^ me) >> 2) & 3
        which = jnp.where(d == 0, (((o ^ q) >> 1) & 1) + 2 * ((o ^ q) & 1), 3 + d)
        if last:
            which = jnp.where((o >> 4) == (me >> 4), which, 7)
        out_ref[i * ENTRY] = which
        out_ref[i * ENTRY + 1] = slot_ref[block]
        out_ref[i * ENTRY + 2] = line

    for n in range(1, 4):
        for t in range(2):
            put((n - 1) * 2 + t, (((y & 3) ^ n) + 4 * t) * GROUP + q, t)
    put(6, me ^ 16, (me >> 4) ^ 1)
    put(7, me, me >> 4, True)
    for i in range(8):
        block = block_ref[i]
        out_ref[RETURN + 3 * i] = ((block ^ me) >> 2) & 1
        out_ref[RETURN + 3 * i + 1] = (((block ^ me) >> 4) & 1) + 2 * (((block ^ me) >> 3) & 1)
        out_ref[RETURN + 3 * i + 2] = jnp.where(block < 0, -1, (block ^ me) & 3)


def columns(place, rows, size):
    first = place * rows // LANES
    return [pl.multiple_of((first + n) % (size // LANES) * LANES, LANES) for n in range(size // LANES - 1)]


def keep_kernel(place_ref, held_ref, held_z_ref, kept_ref):
    capacity, rows, size = held_ref.shape
    for n, column in enumerate(columns(place_ref[0], rows, size)):
        for i, held in enumerate((held_ref, held_z_ref)):
            for j in range(capacity):
                kept_ref[i, j, :, n * LANES : (n + 1) * LANES] = held[j, :, pl.ds(column, LANES)]


def pick(table_ref, entry, kept_ref, core_ref, near=(), far=()):
    which, slot, line = (table_ref[entry * ENTRY + i] for i in range(ENTRY))
    options = [k[i, slot] for k in (kept_ref, core_ref) for i in range(2)]
    return choose(which, options + [g[line] for g in near] + [g[...] for g in far])


def near_kernel(table_ref, kept_ref, core_ref, *outs):
    for n, out in enumerate(outs):
        for t in range(2):
            out[t] = pick(table_ref, n * 2 + t, kept_ref, core_ref)


def far_kernel(table_ref, kept_ref, core_ref, near1, near2, near3, out_ref):
    out_ref[...] = pick(table_ref, 6, kept_ref, core_ref, (near1, near2, near3))


def packed_rows(rows, size):
    return 2 * rows + rows // 2 + size // LANES * rows


def stat_kernel(table_ref, place_ref, sums_ref, kept_ref, core_ref, *refs):
    wide_ref, gram_ref, stat_ref, both_ref = refs[4:]
    _, rows, size = gram_ref.shape
    sums = jnp.sum(sums_ref[...], axis=0)
    gram_ref[0] = sums[:rows]
    for n, column in enumerate(columns(place_ref[0], rows, size)):
        stat_ref[:, n * LANES : (n + 1) * LANES] = gram_ref[0, :, pl.ds(column, LANES)]
    stat = stat_ref[...] + pick(table_ref, 7, kept_ref, core_ref, refs[:3], refs[3:4])
    both_ref[:rows] = stat[:, :LANES]
    both_ref[rows : 2 * rows] = stat[:, LANES : 2 * LANES]
    x, z = place_ref[0] % ACROSS, place_ref[0] // ACROSS
    third = [stat[:, 2 * LANES + s * rows : 2 * LANES + (s + 1) * rows] for s in range(LANES // rows)]
    odd = (x + z // 2) % 2
    half = jnp.where(odd == 0, jnp.concatenate(third[::2], axis=1), jnp.concatenate(third[1::2], axis=1))
    half = jnp.concatenate([half[: rows // 2], half[rows // 2 :]], axis=1)
    start = 2 * rows + rows // 2
    both_ref[2 * rows : start] = half
    for m in range(size // LANES):
        both_ref[start + m * rows : start + (m + 1) * rows] = sums[rows:, m * LANES : (m + 1) * LANES]
    wide_ref[...] = jnp.broadcast_to(both_ref[...][None], wide_ref.shape)


def stack_kernel(first_ref, second_ref, out_ref):
    half = out_ref.shape[0] // 2
    out_ref[:half] = first_ref[...]
    out_ref[half:] = second_ref[...]


def return_kernel(table_ref, line_ref, far_ref, *outs):
    for i in range(8):
        n, line = table_ref[RETURN + 3 * i], table_ref[RETURN + 3 * i + 1]
        outs[i // 2][i % 2] = choose(n, [line_ref[line], far_ref[line]])


def state_kernel(table_ref, state_ref, got0, got1, got2, got3, after_ref, out_ref):
    del after_ref
    for j in range(2):
        way = table_ref[RETURN + 3 * j + 2]
        gram = choose(way, [got0[j], got1[j], got2[j], got3[j]])
        out_ref[j] = state_ref[j] + jnp.where(way >= 0, gram, 0.0)


def split(a):
    high = a.astype(bf16)
    return high, (a - high.astype(f32)).astype(bf16)


def product(a, b):
    (a_high, a_low), (b_high, b_low) = a, b
    half = a_high.shape[0] // 2
    left = jnp.concatenate([a_high, a_high, a_low], axis=1)
    right = jnp.concatenate([b_high, b_low, b_high], axis=0)
    top = jnp.dot(left[:half], right, preferred_element_type=f32)
    corner = jnp.dot(left[half:], right[:, half:], preferred_element_type=f32)
    return jnp.concatenate([top, jnp.concatenate([top[:, half:].T, corner], axis=1)], axis=0)


def copies_kernel(part_ref, after_ref, out_ref, sems):
    del after_ref
    copies = [pltpu.make_async_copy(part_ref, out_ref.at[x], sems.at[x]) for x in range(out_ref.shape[0])]
    for copy in copies:
        copy.start()
    for copy in copies:
        copy.wait()


def thin_product(a, b):
    a_high, a_low = split(a)
    rows = a.shape[0]
    both = jnp.dot(jnp.concatenate([a_high, a_low], axis=0), b[0], preferred_element_type=f32)
    return both[:rows] + (both[rows:] + jnp.dot(a_high, b[1], preferred_element_type=f32))


def newton_kernel(count, place_ref, all_ref, after_ref, out_ref, end_ref, stat_ref):
    del after_ref
    end_ref[...] = jnp.zeros_like(end_ref)
    xs, zs, _, _ = all_ref.shape
    size = stat_ref.shape[1]
    rows = size // (xs * zs)
    start = 2 * rows + rows // 2
    place = place_ref[0]
    block = lambda i: slice(i % zs * LANES, (i % zs + 1) * LANES)
    third = []
    for z in range(zs):
        for n in range(2):
            part = jnp.concatenate([all_ref[x, z, n * rows : (n + 1) * rows] for x in range(xs)], axis=0)
            stat_ref[block(z), block(z + n)] = part
            if n == 1:
                stat_ref[block(z + n), block(z)] = part.T
        strips = []
        for x in range(xs):
            half = all_ref[x, z, 2 * rows : start]
            half = jnp.concatenate([half[:, : LANES // 2], half[:, LANES // 2 :]], axis=0)
            blank = jnp.zeros((rows, rows), f32)
            pieces = [half[:, :rows], blank, half[:, rows:], blank]
            strips.append(jnp.concatenate(pieces if (x + z // 2) % 2 == 0 else pieces[1:2] + pieces[:1] + pieces[3:] + pieces[2:3], axis=1))
        third.append(jnp.concatenate(strips, axis=0))
    for z in range(zs // 2):
        part = third[z] + third[z + 2].T
        stat_ref[block(z), block(z + 2)] = part
        stat_ref[block(z + 2), block(z)] = part.T
    stat = stat_ref[...]
    diagonal = lax.broadcasted_iota(jnp.int32, (size, size), 0) == lax.broadcasted_iota(jnp.int32, (size, size), 1)
    plus = lambda a, m: jnp.where(diagonal, m + a, m)
    thin_rows = lax.broadcasted_iota(jnp.int32, (rows, size), 0) + place * rows
    thin_cols = lax.broadcasted_iota(jnp.int32, (rows, size), 1)
    thin_eye = (thin_rows == thin_cols).astype(f32)
    squares = jnp.sum(stat * stat)
    trace = jnp.sum(jnp.where(diagonal, stat, 0.0))
    norm = jnp.sqrt(squares)
    damp = DAMP * norm
    scale = jnp.sqrt(squares + 2.0 * damp * trace + size * damp * damp)
    iterate = plus(damp, stat) * (1.0 / scale)
    mine = stat_ref[pl.ds(pl.multiple_of(place * rows, rows), rows), :]
    mine = (mine + damp * thin_eye) * (1.0 / scale)
    thin = 1.25 * thin_eye - 0.25 * mine
    parts_of = split(iterate)
    for _ in range(ITERS - 2):
        square = product(parts_of, parts_of)
        factor2 = split(plus(1.5625, 0.0625 * square - 0.625 * iterate))
        iterate = product(parts_of, split(product(factor2, factor2)))
        parts_of = split(iterate)
        thin = 1.25 * thin - 0.25 * thin_product(thin, parts_of)
    last = thin_product(thin, parts_of)
    for _ in range(4):
        last = 1.25 * last - 0.25 * thin_product(last, parts_of)
    thin = (1.25 * thin - 0.25 * last) * jnp.exp(-0.25 * jnp.log(scale))
    mean = [
        jnp.concatenate(
            [all_ref[x, z, start + m * rows : start + (m + 1) * rows] for z in range(zs) for x in range(xs)], axis=0
        )
        for m in range(size // LANES)
    ]
    mean = (jnp.concatenate(mean, axis=1) * (1.0 / count)).astype(bf16)
    out_ref[0] = jnp.dot(thin.astype(bf16), mean, preferred_element_type=f32).astype(bf16)


def body(grads, owner, state):
    local = grads[:, 0]
    shards, size, _ = local.shape
    held = state[0]
    capacity, rows, _ = held.shape
    reps = lax.axis_size("rep")
    blocks = owner.shape[0]
    groups = blocks // GROUP
    shape = lambda *s: jax.ShapeDtypeStruct(s, f32)

    def across(x, k):
        return lax.ppermute(x, "pre", [(i, i ^ k) for i in range(blocks)])

    zs = reps // ACROSS
    x_groups = [[z * ACROSS + x for x in range(ACROSS)] for z in range(zs)]
    z_groups = [[z * ACROSS + x for z in range(zs)] for x in range(ACROSS)]

    def exchange(x, which):
        return lax.all_to_all(x, "rep", 0, 0, tiled=True, axis_index_groups=which)

    me = lax.axis_index("pre").reshape(1).astype(jnp.int32)
    place = lax.axis_index("rep").reshape(1).astype(jnp.int32)
    table = pl.pallas_call(
        table_kernel,
        out_shape=jax.ShapeDtypeStruct((RETURN + 24,), jnp.int32),
        in_specs=[SMEM, SMEM],
        out_specs=SMEM,
        scratch_shapes=[
            pltpu.SMEM((blocks,), jnp.int32),
            pltpu.SMEM((blocks,), jnp.int32),
            pltpu.SMEM((16,), jnp.int32),
        ],
    )(me, owner)

    held_z = across(held, 2)
    sums = call(
        gram_kernel,
        shape(ACROSS, zs, 2 * rows, size),
        [VMEM],
        (2 * shards * size**3, 4 * size * size * (shards + 2)),
        local,
        limit=62,
        out_specs=ANY,
        scratch=[
            pltpu.VMEM((ACROSS, zs, 2 * rows, size), f32),
            pltpu.SemaphoreType.DMA((2, ACROSS)),
        ],
    )
    sums = exchange(sums, x_groups)
    kept = call(
        keep_kernel,
        shape(2, capacity, rows, size - LANES),
        [SMEM, VMEM, VMEM],
        (2 * 100 * size**3, 4 * size * rows * 8),
        place,
        held,
        held_z,
    )
    core = across(kept, 1)
    near = call(
        near_kernel,
        [shape(2, rows, size - LANES)] * 3,
        [SMEM, VMEM, VMEM],
        (0, 4 * size * rows * 12),
        table,
        kept,
        core,
    )
    near = [across(sent, GROUP * (n + 1)) for n, sent in enumerate(near)]
    far = call(
        far_kernel,
        shape(rows, size - LANES),
        [SMEM] + [VMEM] * 5,
        (0, 4 * size * rows * 12),
        table,
        kept,
        core,
        *near,
    )
    sums = call(
        sum_kernel,
        shape(zs, 2 * rows, size),
        [VMEM, ANY],
        (0, 4 * size * rows * 40),
        sums,
        far,
    )
    sums = exchange(sums, z_groups)
    far = across(far, 4 * GROUP)
    both, gram = call(
        stat_kernel,
        [shape(zs, packed_rows(rows, size), LANES), shape(1, rows, size)],
        [SMEM, SMEM] + [VMEM] * 7,
        (0, 4 * size * rows * 45),
        table,
        place,
        sums,
        kept,
        core,
        *near,
        far,
        scratch=[
            pltpu.VMEM((rows, size - LANES), f32),
            pltpu.VMEM((packed_rows(rows, size), LANES), f32),
        ],
    )
    both = exchange(both, z_groups)
    line = gram
    lines = []
    for bit in (4, 2):
        line = call(
            stack_kernel,
            shape(2 * line.shape[0], rows, size),
            [VMEM] * 2,
            (2 * (60 if bit == 2 else 0) * size**3, 4 * size * rows * 8),
            line,
            across(line, GROUP * bit),
        )
        lines.append(line)
    both = call(
        copies_kernel,
        shape(ACROSS, zs, packed_rows(rows, size), LANES),
        [VMEM, ANY],
        (0, 4 * size * rows * 40),
        both,
        lines[0],
        out_specs=HBM,
        scratch=[pltpu.SemaphoreType.DMA((ACROSS,))],
    )
    both = exchange(both, x_groups)
    own, *sent = call(
        return_kernel,
        [shape(capacity, rows, size)] * 4,
        [SMEM] + [VMEM] * 2,
        (0, 4 * size * rows * 24),
        table,
        line,
        across(line, GROUP),
    )
    count = shards * reps
    update, end = call(
        functools.partial(newton_kernel, count),
        [jax.ShapeDtypeStruct((1, rows, size), bf16), shape(8, LANES)],
        [SMEM, VMEM, ANY],
        (2 * 20 * size**3, 8 * size * size),
        place,
        both,
        own,
        scratch=[pltpu.VMEM((size, size), f32)],
    )
    new_state = call(
        state_kernel,
        shape(capacity, rows, size),
        [SMEM] + [VMEM] * 5 + [ANY],
        (0, 4 * size * rows * 8),
        table,
        held,
        own,
        *[across(rows_sent, k + 1) for k, rows_sent in enumerate(sent)],
        end,
    )
    return (new_state[None], update)


def solution(mesh):
    placed = (P("rep", "pre", None, None), P(), P("pre", None, "rep", None))
    return jax.shard_map(
        body,
        mesh=mesh,
        in_specs=placed,
        out_specs=(P("pre", None, "rep", None), P("pre", "rep", None)),
        check_vma=False,
    )
```

```python
import functools

import jax
import jax.numpy as jnp
from jax import lax
from jax.experimental import pallas as pl
from jax.experimental.pallas import tpu as pltpu
from jax.sharding import PartitionSpec as P

ITERS = 4
DAMP = 0.05
GROUP = 4
LANES = 128
ENTRY = 3
RETURN = 8 * ENTRY
ACROSS = 4
f32 = jnp.float32
bf16 = jnp.bfloat16

VMEM = pl.BlockSpec(memory_space=pltpu.VMEM)
ANY = pl.BlockSpec(memory_space=pl.ANY)
HBM = pl.BlockSpec(memory_space=pltpu.HBM)
SMEM = pl.BlockSpec(memory_space=pltpu.SMEM)


def call(kernel, out_shape, in_specs, cost, *args, scratch=(), out_specs=VMEM, limit=40):
    multiple = isinstance(out_shape, (list, tuple))
    return pl.pallas_call(
        kernel,
        out_shape=out_shape,
        in_specs=in_specs,
        out_specs=[out_specs] * len(out_shape) if multiple else out_specs,
        scratch_shapes=list(scratch),
        compiler_params=pltpu.CompilerParams(vmem_limit_bytes=limit * 2**20),
        cost_estimate=pl.CostEstimate(flops=cost[0], bytes_accessed=cost[1], transcendentals=0),
    )(*args)


def gram_kernel(grads_ref, out_ref, whole_ref, out_sems):
    shards, size, _ = grads_ref.shape
    xs, zs, double, _ = out_ref.shape
    rows = double // 2
    stores = []
    half = size // 2
    for h in range(2):
        gram = None
        total = None
        for s in range(shards):
            mine = grads_ref[s, h * half : (h + 1) * half]
            term = lax.dot_general(mine, grads_ref[s], (((1,), (1,)), ((), ())), preferred_element_type=f32)
            gram = term if gram is None else gram + term
            wide = mine.astype(f32)
            total = wide if total is None else total + wide
        gram = gram.reshape(zs // 2, xs, rows, size)
        total = total.reshape(zs // 2, xs, rows, size)
        part = slice(h * zs // 2, (h + 1) * zs // 2)
        for x in range(xs):
            whole_ref[x, part, :rows, :] = gram[:, x]
            whole_ref[x, part, rows:, :] = total[:, x]
            stores.append(pltpu.make_async_copy(whole_ref.at[x, part], out_ref.at[x, part], out_sems.at[h, x]))
            stores[-1].start()
    for store in stores:
        store.wait()


def sum_kernel(parts_ref, after_ref, out_ref):
    del after_ref
    out_ref[...] = jnp.sum(parts_ref[...], axis=0)


def choose(k, options):
    value = options[0]
    for i in range(1, len(options)):
        value = jnp.where(k == i, options[i], value)
    return value


def table_kernel(me_ref, owner_ref, out_ref, count_ref, slot_ref, block_ref):
    blocks = owner_ref.shape[0]
    me = me_ref[0]
    y, q = me >> 2, me & 3
    for b in range(blocks):
        count_ref[b] = 0
    for i in range(9):
        block_ref[i] = -1
    for b in range(blocks):
        o = owner_ref[b]
        s = jnp.minimum(count_ref[o], 1)
        count_ref[o] = s + 1
        slot_ref[b] = s
        near = o ^ me
        block_ref[jnp.where(near < 4, near * 2 + s, 8)] = b

    def put(i, block, line, last=False):
        o = owner_ref[block]
        d = ((o ^ me) >> 2) & 3
        which = jnp.where(d == 0, (((o ^ q) >> 1) & 1) + 2 * ((o ^ q) & 1), 3 + d)
        if last:
            which = jnp.where((o >> 4) == (me >> 4), which, 7)
        out_ref[i * ENTRY] = which
        out_ref[i * ENTRY + 1] = slot_ref[block]
        out_ref[i * ENTRY + 2] = line

    for n in range(1, 4):
        for t in range(2):
            put((n - 1) * 2 + t, (((y & 3) ^ n) + 4 * t) * GROUP + q, t)
    put(6, me ^ 16, (me >> 4) ^ 1)
    put(7, me, me >> 4, True)
    for i in range(8):
        block = block_ref[i]
        out_ref[RETURN + 3 * i] = ((block ^ me) >> 2) & 1
        out_ref[RETURN + 3 * i + 1] = (((block ^ me) >> 4) & 1) + 2 * (((block ^ me) >> 3) & 1)
        out_ref[RETURN + 3 * i + 2] = jnp.where(block < 0, -1, (block ^ me) & 3)


def columns(place, rows, size):
    first = place * rows // LANES
    return [pl.multiple_of((first + n) % (size // LANES) * LANES, LANES) for n in range(size // LANES - 1)]


def keep_kernel(place_ref, held_ref, held_z_ref, kept_ref):
    capacity, rows, size = held_ref.shape
    for n, column in enumerate(columns(place_ref[0], rows, size)):
        for i, held in enumerate((held_ref, held_z_ref)):
            for j in range(capacity):
                kept_ref[i, j, :, n * LANES : (n + 1) * LANES] = held[j, :, pl.ds(column, LANES)]


def pick(table_ref, entry, kept_ref, core_ref, near=(), far=()):
    which, slot, line = (table_ref[entry * ENTRY + i] for i in range(ENTRY))
    options = [k[i, slot] for k in (kept_ref, core_ref) for i in range(2)]
    return choose(which, options + [g[line] for g in near] + [g[...] for g in far])


def near_kernel(table_ref, kept_ref, core_ref, *outs):
    for n, out in enumerate(outs):
        for t in range(2):
            out[t] = pick(table_ref, n * 2 + t, kept_ref, core_ref)


def far_kernel(table_ref, kept_ref, core_ref, near1, near2, near3, out_ref):
    out_ref[...] = pick(table_ref, 6, kept_ref, core_ref, (near1, near2, near3))


def packed_rows(rows, size):
    return 2 * rows + rows // 2 + size // LANES * rows


def stat_kernel(table_ref, place_ref, sums_ref, kept_ref, core_ref, *refs):
    wide_ref, gram_ref, stat_ref, both_ref = refs[4:]
    _, rows, size = gram_ref.shape
    sums = jnp.sum(sums_ref[...], axis=0)
    gram_ref[0] = sums[:rows]
    for n, column in enumerate(columns(place_ref[0], rows, size)):
        stat_ref[:, n * LANES : (n + 1) * LANES] = gram_ref[0, :, pl.ds(column, LANES)]
    stat = stat_ref[...] + pick(table_ref, 7, kept_ref, core_ref, refs[:3], refs[3:4])
    both_ref[:rows] = stat[:, :LANES]
    both_ref[rows : 2 * rows] = stat[:, LANES : 2 * LANES]
    x, z = place_ref[0] % ACROSS, place_ref[0] // ACROSS
    third = [stat[:, 2 * LANES + s * rows : 2 * LANES + (s + 1) * rows] for s in range(LANES // rows)]
    odd = (x + z // 2) % 2
    half = jnp.where(odd == 0, jnp.concatenate(third[::2], axis=1), jnp.concatenate(third[1::2], axis=1))
    half = jnp.concatenate([half[: rows // 2], half[rows // 2 :]], axis=1)
    start = 2 * rows + rows // 2
    both_ref[2 * rows : start] = half
    for m in range(size // LANES):
        both_ref[start + m * rows : start + (m + 1) * rows] = sums[rows:, m * LANES : (m + 1) * LANES]
    wide_ref[...] = jnp.broadcast_to(both_ref[...][None], wide_ref.shape)


def stack_kernel(first_ref, second_ref, out_ref):
    half = out_ref.shape[0] // 2
    out_ref[:half] = first_ref[...]
    out_ref[half:] = second_ref[...]


def return_kernel(table_ref, line_ref, far_ref, *outs):
    for i in range(8):
        n, line = table_ref[RETURN + 3 * i], table_ref[RETURN + 3 * i + 1]
        outs[i // 2][i % 2] = choose(n, [line_ref[line], far_ref[line]])


def state_kernel(table_ref, state_ref, got0, got1, got2, got3, after_ref, out_ref):
    del after_ref
    for j in range(2):
        way = table_ref[RETURN + 3 * j + 2]
        gram = choose(way, [got0[j], got1[j], got2[j], got3[j]])
        out_ref[j] = state_ref[j] + jnp.where(way >= 0, gram, 0.0)


def split(a):
    high = a.astype(bf16)
    return high, (a - high.astype(f32)).astype(bf16)


def product(a, b):
    (a_high, a_low), (b_high, b_low) = a, b
    half = a_high.shape[0] // 2
    left = jnp.concatenate([a_high, a_high, a_low], axis=1)
    right = jnp.concatenate([b_high, b_low, b_high], axis=0)
    top = jnp.dot(left[:half], right, preferred_element_type=f32)
    corner = jnp.dot(left[half:], right[:, half:], preferred_element_type=f32)
    return jnp.concatenate([top, jnp.concatenate([top[:, half:].T, corner], axis=1)], axis=0)


def copies_kernel(part_ref, after_ref, out_ref, sems):
    del after_ref
    copies = [pltpu.make_async_copy(part_ref, out_ref.at[x], sems.at[x]) for x in range(out_ref.shape[0])]
    for copy in copies:
        copy.start()
    for copy in copies:
        copy.wait()


def thin_product(a, b):
    a_high, a_low = split(a)
    rows = a.shape[0]
    both = jnp.dot(jnp.concatenate([a_high, a_low], axis=0), b[0], preferred_element_type=f32)
    return both[:rows] + (both[rows:] + jnp.dot(a_high, b[1], preferred_element_type=f32))


def newton_kernel(count, place_ref, all_ref, after_ref, out_ref, end_ref, stat_ref):
    del after_ref
    end_ref[...] = jnp.zeros_like(end_ref)
    xs, zs, _, _ = all_ref.shape
    size = stat_ref.shape[1]
    rows = size // (xs * zs)
    start = 2 * rows + rows // 2
    place = place_ref[0]
    block = lambda i: slice(i % zs * LANES, (i % zs + 1) * LANES)
    third = []
    for z in range(zs):
        for n in range(2):
            part = jnp.concatenate([all_ref[x, z, n * rows : (n + 1) * rows] for x in range(xs)], axis=0)
            stat_ref[block(z), block(z + n)] = part
            if n == 1:
                stat_ref[block(z + n), block(z)] = part.T
        strips = []
        for x in range(xs):
            half = all_ref[x, z, 2 * rows : start]
            half = jnp.concatenate([half[:, : LANES // 2], half[:, LANES // 2 :]], axis=0)
            blank = jnp.zeros((rows, rows), f32)
            pieces = [half[:, :rows], blank, half[:, rows:], blank]
            strips.append(jnp.concatenate(pieces if (x + z // 2) % 2 == 0 else pieces[1:2] + pieces[:1] + pieces[3:] + pieces[2:3], axis=1))
        third.append(jnp.concatenate(strips, axis=0))
    for z in range(zs // 2):
        part = third[z] + third[z + 2].T
        stat_ref[block(z), block(z + 2)] = part
        stat_ref[block(z + 2), block(z)] = part.T
    stat = stat_ref[...]
    diagonal = lax.broadcasted_iota(jnp.int32, (size, size), 0) == lax.broadcasted_iota(jnp.int32, (size, size), 1)
    plus = lambda a, m: jnp.where(diagonal, m + a, m)
    thin_rows = lax.broadcasted_iota(jnp.int32, (rows, size), 0) + place * rows
    thin_cols = lax.broadcasted_iota(jnp.int32, (rows, size), 1)
    thin_eye = (thin_rows == thin_cols).astype(f32)
    squares = jnp.sum(stat * stat)
    trace = jnp.sum(jnp.where(diagonal, stat, 0.0))
    norm = jnp.sqrt(squares)
    damp = DAMP * norm
    scale = jnp.sqrt(squares + 2.0 * damp * trace + size * damp * damp)
    iterate = plus(damp, stat) * (1.0 / scale)
    mine = stat_ref[pl.ds(pl.multiple_of(place * rows, rows), rows), :]
    mine = (mine + damp * thin_eye) * (1.0 / scale)
    thin = 1.25 * thin_eye - 0.25 * mine
    parts_of = split(iterate)
    for _ in range(ITERS - 2):
        square = product(parts_of, parts_of)
        factor2 = split(plus(1.5625, 0.0625 * square - 0.625 * iterate))
        iterate = product(parts_of, split(product(factor2, factor2)))
        parts_of = split(iterate)
        thin = 1.25 * thin - 0.25 * thin_product(thin, parts_of)
    last = thin_product(thin, parts_of)
    for _ in range(4):
        last = 1.25 * last - 0.25 * thin_product(last, parts_of)
    thin = (1.25 * thin - 0.25 * last) * jnp.exp(-0.25 * jnp.log(scale))
    mean = [
        jnp.concatenate(
            [
                (all_ref[x, z, start + m * rows : start + (m + 1) * rows] * (1.0 / count)).astype(bf16)
                for z in range(zs)
                for x in range(xs)
            ],
            axis=0,
        )
        for m in range(size // LANES)
    ]
    mean = jnp.concatenate(mean, axis=1)
    out_ref[0] = jnp.dot(thin.astype(bf16), mean, preferred_element_type=f32).astype(bf16)


def body(grads, owner, state):
    local = grads[:, 0]
    shards, size, _ = local.shape
    held = state[0]
    capacity, rows, _ = held.shape
    reps = lax.axis_size("rep")
    blocks = owner.shape[0]
    groups = blocks // GROUP
    shape = lambda *s: jax.ShapeDtypeStruct(s, f32)

    def across(x, k):
        return lax.ppermute(x, "pre", [(i, i ^ k) for i in range(blocks)])

    zs = reps // ACROSS
    x_groups = [[z * ACROSS + x for x in range(ACROSS)] for z in range(zs)]
    z_groups = [[z * ACROSS + x for z in range(zs)] for x in range(ACROSS)]

    def exchange(x, which):
        return lax.all_to_all(x, "rep", 0, 0, tiled=True, axis_index_groups=which)

    me = lax.axis_index("pre").reshape(1).astype(jnp.int32)
    place = lax.axis_index("rep").reshape(1).astype(jnp.int32)
    table = pl.pallas_call(
        table_kernel,
        out_shape=jax.ShapeDtypeStruct((RETURN + 24,), jnp.int32),
        in_specs=[SMEM, SMEM],
        out_specs=SMEM,
        scratch_shapes=[
            pltpu.SMEM((blocks,), jnp.int32),
            pltpu.SMEM((blocks,), jnp.int32),
            pltpu.SMEM((16,), jnp.int32),
        ],
    )(me, owner)

    held_z = across(held, 2)
    sums = call(
        gram_kernel,
        shape(ACROSS, zs, 2 * rows, size),
        [VMEM],
        (2 * shards * size**3, 4 * size * size * (shards + 2)),
        local,
        limit=62,
        out_specs=ANY,
        scratch=[
            pltpu.VMEM((ACROSS, zs, 2 * rows, size), f32),
            pltpu.SemaphoreType.DMA((2, ACROSS)),
        ],
    )
    sums = exchange(sums, x_groups)
    kept = call(
        keep_kernel,
        shape(2, capacity, rows, size - LANES),
        [SMEM, VMEM, VMEM],
        (2 * 100 * size**3, 4 * size * rows * 8),
        place,
        held,
        held_z,
    )
    core = across(kept, 1)
    near = call(
        near_kernel,
        [shape(2, rows, size - LANES)] * 3,
        [SMEM, VMEM, VMEM],
        (0, 4 * size * rows * 12),
        table,
        kept,
        core,
    )
    near = [across(sent, GROUP * (n + 1)) for n, sent in enumerate(near)]
    far = call(
        far_kernel,
        shape(rows, size - LANES),
        [SMEM] + [VMEM] * 5,
        (0, 4 * size * rows * 12),
        table,
        kept,
        core,
        *near,
    )
    sums = call(
        sum_kernel,
        shape(zs, 2 * rows, size),
        [VMEM, ANY],
        (0, 4 * size * rows * 40),
        sums,
        far,
    )
    sums = exchange(sums, z_groups)
    far = across(far, 4 * GROUP)
    both, gram = call(
        stat_kernel,
        [shape(zs, packed_rows(rows, size), LANES), shape(1, rows, size)],
        [SMEM, SMEM] + [VMEM] * 7,
        (0, 4 * size * rows * 45),
        table,
        place,
        sums,
        kept,
        core,
        *near,
        far,
        scratch=[
            pltpu.VMEM((rows, size - LANES), f32),
            pltpu.VMEM((packed_rows(rows, size), LANES), f32),
        ],
    )
    both = exchange(both, z_groups)
    line = gram
    lines = []
    for bit in (4, 2):
        line = call(
            stack_kernel,
            shape(2 * line.shape[0], rows, size),
            [VMEM] * 2,
            (2 * (60 if bit == 2 else 0) * size**3, 4 * size * rows * 8),
            line,
            across(line, GROUP * bit),
        )
        lines.append(line)
    both = call(
        copies_kernel,
        shape(ACROSS, zs, packed_rows(rows, size), LANES),
        [VMEM, ANY],
        (0, 4 * size * rows * 40),
        both,
        lines[0],
        out_specs=HBM,
        scratch=[pltpu.SemaphoreType.DMA((ACROSS,))],
    )
    both = exchange(both, x_groups)
    own, *sent = call(
        return_kernel,
        [shape(capacity, rows, size)] * 4,
        [SMEM] + [VMEM] * 2,
        (0, 4 * size * rows * 24),
        table,
        line,
        across(line, GROUP),
    )
    count = shards * reps
    update, end = call(
        functools.partial(newton_kernel, count),
        [jax.ShapeDtypeStruct((1, rows, size), bf16), shape(8, LANES)],
        [SMEM, VMEM, ANY],
        (2 * 20 * size**3, 8 * size * size),
        place,
        both,
        own,
        scratch=[pltpu.VMEM((size, size), f32)],
    )
    new_state = call(
        state_kernel,
        shape(capacity, rows, size),
        [SMEM] + [VMEM] * 5 + [ANY],
        (0, 4 * size * rows * 8),
        table,
        held,
        own,
        *[across(rows_sent, k + 1) for k, rows_sent in enumerate(sent)],
        end,
    )
    return (new_state[None], update)


def solution(mesh):
    placed = (P("rep", "pre", None, None), P(), P("pre", None, "rep", None))
    return jax.shard_map(
        body,
        mesh=mesh,
        in_specs=placed,
        out_specs=(P("pre", None, "rep", None), P("pre", "rep", None)),
        check_vma=False,
    )
```
